32 devices in a mesh: gx: 16 (over z, x, core), gy: 2 (over y).
Axes of the slice: x: 2, y: 2, z: 4, core: 2. Of those that a mesh axis runs over, the one named last changes fastest.
Arguments:
- elevation: float32 [2048, 1, 2, 128], P('gx', None, 'gy'), may hold values from -0.4 to 0.4
- velocity: float32 [2, 2048, 1, 2, 128], P(None, 'gx', None, 'gy'), may hold values from -2 to 2
- depth: float32 [2048, 1, 2, 128], P('gx', None, 'gy'), may hold values from 3 to 6
- turbine: float32 [2048, 1, 2, 128], P('gx', None, 'gy'), may hold values from 0.1 to 2
- wet_tiles: int32 [16, 1, 2], P('gx', None, 'gy'), may hold values 0 or 1
- farm: int32 [2048, 1, 2, 128], P('gx', None, 'gy'), may hold values from 0 to 31, as said below
Outputs:
- adjoint: float32 [3, 2048, 1, 2, 128], P(None, 'gx', None, 'gy')
- turbine_grad: float32 [2048, 1, 2, 128], P('gx', None, 'gy')
- farm_grad: float32 [32], P(('gx', 'gy'))
The draws below stay inside these ranges and needn't reach their ends.
Inputs may be any that keep to these rules, and one draw needn't show every extreme that they name: A cell in tile row i, in a tile column of group j (its column modulo 2), belongs to farm i * 2 + j or to farm ((i + 1) mod 16) * 2 + j.
All inputs are finite; a program needn't handle non-finite values. No bound on the sum of `wet_tiles` on one device may be relied on, other than what follows from the above.
Results may differ from the reference program's by a relative error of at most 0.0002.
Values sent between devices are 32-bit elements; how exact they have to be, the bound alone decides.
No kernel may reach another device: no remote copies, remote signals or barrier semaphores. Data moves between devices by JAX's collectives and lax.ppermute only.
A program may use at most 64 MiB of HBM per device.

```python
import math
import jax
import jax.numpy as jnp
from jax import lax

TILE = 128
TYL = 1
TROWS = 16
YGROUPS = 2
NX = 2048
FARMS = 32


def draw_farm(key, part):
    array_shape = (NX, TYL, YGROUPS, TILE)
    step_up = jax.random.randint(key, array_shape, 0, 2)
    row_group = lax.broadcasted_iota(jnp.int32, array_shape, 0) // TILE
    column_group = lax.broadcasted_iota(jnp.int32, array_shape, 2)
    return ((row_group + step_up) % TROWS * YGROUPS + column_group).astype(jnp.int32)


def place_ends(values, key, low, high):
    place = [jax.random.randint(jax.random.fold_in(key, axis), (), 0, length) for axis, length in enumerate(values.shape)]
    main_axis = values.shape.index(max(values.shape))
    beside = place[:main_axis] + [(place[main_axis] + 1) % values.shape[main_axis]] + place[main_axis + 1:]
    return values.at[tuple(place)].set(low).at[tuple(beside)].set(high)


def shard_levels(stream_key, extent, cuts, low, high):
    loudness = 1.0
    for position, blocks in cuts:
        steps = jax.random.uniform(jax.random.fold_in(jax.random.fold_in(stream_key, 6), position), (blocks,), jnp.float32, low / len(cuts), high / len(cuts))
        loudness = loudness * jnp.repeat(jnp.exp(steps), extent[position] // blocks).reshape((-1,) + (1,) * (len(extent) - 1 - position))
    return loudness


def normal_values(rng, extent, spread, bound, split=(), kind=jnp.bfloat16):
    factor_of = shard_levels(rng, extent, split, -0.22, 0.18) if split else 1.0
    values = jax.random.normal(rng, extent, jnp.float32) * spread * factor_of
    return jnp.minimum(jnp.maximum(values, -bound), bound).astype(kind)


def setup_inputs(seed: int = 0) -> dict:
    keys = jax.random.split(jax.random.key(seed), 7)
    elevation = jnp.clip(jax.random.uniform(keys[0], (NX, TYL, YGROUPS, TILE), jnp.float32, -0.4, 0.4) * shard_levels(keys[0], (NX, TYL, YGROUPS, TILE), ((0, 16), (2, 2)), -0.4, 0.0), -0.4, 0.4)
    velocity = normal_values(keys[1], (2, NX, TYL, YGROUPS, TILE), 0.5, 2.0, ((1, 16), (3, 2)), jnp.float32)
    depth = jnp.clip(3.0 + 3.0 * jax.random.uniform(keys[2], (NX, TYL, YGROUPS, TILE), jnp.float32) ** shard_levels(keys[2], (NX, TYL, YGROUPS, TILE), ((0, 16), (2, 2)), -0.2, 0.2), 3.0, 6.0)
    turbine = jnp.clip(jnp.exp(math.log(2.0) - 2.9957323 * jax.random.uniform(keys[3], (NX, TYL, YGROUPS, TILE), jnp.float32) ** shard_levels(keys[3], (NX, TYL, YGROUPS, TILE), ((0, 16), (2, 2)), -0.2, 0.2)), 0.1, 2.0)
    wet_tiles = place_ends((jax.random.randint(keys[4], (TROWS, TYL, YGROUPS), 0, 4) < 3).astype(jnp.int32), jax.random.fold_in(keys[4], 1), 0, 1)
    farm = draw_farm(jax.random.fold_in(keys[6], 71), 0)
    return {"elevation": elevation, "velocity": velocity, "depth": depth, "turbine": turbine, "wet_tiles": wet_tiles, "farm": farm}


ADVECT = 0.1
GRAVITY = 0.3
FRICTION = 0.5
BED_DRAG = 0.1
HYPERVISC = 0.004
SPEED_EPS = 0.01

def window(field, shift_x, shift_y):
    extent_x = field.shape[-3]
    extent_y = field.shape[-1]
    return field[..., 2 + shift_x:extent_x - 2 + shift_x, :, 2 + shift_y:extent_y - 2 + shift_y]

def along_x(field):
    return (window(field, -2, 0) - 8.0 * window(field, -1, 0) + 8.0 * window(field, 1, 0) - window(field, 2, 0)) / 12.0

def along_y(field):
    return (window(field, 0, -2) - 8.0 * window(field, 0, -1) + 8.0 * window(field, 0, 1) - window(field, 0, 2)) / 12.0

def biharmonic(field):
    nearest = window(field, 1, 0) + window(field, -1, 0) + window(field, 0, 1) + window(field, 0, -1)
    diagonal = window(field, 1, 1) + window(field, 1, -1) + window(field, -1, 1) + window(field, -1, -1)
    distant = window(field, 2, 0) + window(field, -2, 0) + window(field, 0, 2) + window(field, 0, -2)
    return 20.0 * window(field, 0, 0) - 8.0 * nearest + 2.0 * diagonal + distant

def tendency(padded, ground, drag_field):
    height = padded[0]
    east = padded[1]
    north = padded[2]
    column = ground + height
    centre_u = window(east, 0, 0)
    centre_v = window(north, 0, 0)
    centre_h = window(column, 0, 0)
    speed = jnp.sqrt(centre_u * centre_u + centre_v * centre_v + SPEED_EPS)
    damping = FRICTION * (BED_DRAG + drag_field) * speed / centre_h
    rate_h = -ADVECT * (along_x(column * east) + along_y(column * north))
    rate_u = -ADVECT * (centre_u * along_x(east) + centre_v * along_y(east)) - GRAVITY * along_x(height) - damping * centre_u - HYPERVISC * biharmonic(east)
    rate_v = -ADVECT * (centre_u * along_x(north) + centre_v * along_y(north)) - GRAVITY * along_y(height) - damping * centre_v - HYPERVISC * biharmonic(north)
    return jnp.stack([rate_h, rate_u, rate_v])

def banded(padded, ground_pad, drag_field):
    bands = drag_field.shape[0] // TILE

    def one_band(index):
        start = index * TILE
        piece = lax.dynamic_slice_in_dim(padded, start, TILE + 4, 1)
        ground = lax.dynamic_slice_in_dim(ground_pad, start, TILE + 4, 0)
        drag_part = lax.dynamic_slice_in_dim(drag_field, start, TILE, 0)
        return tendency(piece, ground, drag_part)
    result = lax.map(jax.checkpoint(one_band), jnp.arange(bands, dtype=jnp.int32))
    return jnp.moveaxis(result, 0, 1).reshape(3, bands * TILE, 1, result.shape[-1])

def surround(state):
    return jnp.pad(state, ((0, 0), (2, 2), (0, 0), (2, 2)))

def advance(state, ground_pad, drag_field, wet):
    first = banded(surround(state), ground_pad, drag_field)
    section_a = wet * (state + first)
    second = banded(surround(section_a), ground_pad, drag_field)
    section_b = wet * (0.75 * state + 0.25 * (section_a + second))
    third = banded(surround(section_b), ground_pad, drag_field)
    return wet * (state / 3.0 + 2.0 / 3.0 * (section_b + third))

def reference(elevation, velocity, depth, turbine, wet_tiles, farm):
    grid_x = elevation.shape[0]
    grid_y = elevation.shape[1] * elevation.shape[2] * elevation.shape[3]
    state = jnp.concatenate([elevation.reshape(1, grid_x, 1, grid_y), velocity.reshape(2, grid_x, 1, grid_y)], axis=0)
    ground_pad = jnp.pad(depth.reshape(grid_x, 1, grid_y), ((2, 2), (0, 0), (2, 2)))
    drag_field = turbine.reshape(grid_x, 1, grid_y)
    wet_rows = jnp.repeat(wet_tiles.astype(jnp.float32), TILE, axis=0)
    wet = jnp.broadcast_to(wet_rows[..., None], elevation.shape).reshape(grid_x, 1, grid_y)
    stepper = jax.checkpoint(advance)

    def objective(start, drag_values):
        middle = stepper(start, ground_pad, drag_values, wet)
        final = stepper(middle, ground_pad, drag_values, wet)
        speed = jnp.sqrt(final[1] * final[1] + final[2] * final[2] + SPEED_EPS)
        return jnp.sum(drag_values * wet * speed * speed * speed)
    state_grad, drag_grad = jax.grad(objective, argnums=(0, 1))(state, drag_field)
    adjoint = state_grad.reshape((3,) + elevation.shape)
    turbine_grad = drag_grad.reshape(elevation.shape)
    totals = jax.ops.segment_sum(turbine_grad.reshape(-1), farm.reshape(-1).astype(jnp.int32), num_segments=FARMS)
    farm_grad = totals / (TILE * TILE * TYL)
    return (adjoint, turbine_grad, farm_grad)
```

```python
import jax
import jax.numpy as jnp
from jax import lax
from jax.experimental import pallas as pl
from jax.experimental.pallas import tpu as pltpu
from jax.sharding import PartitionSpec as P

SPEED_EPS = 0.01
BED_DRAG = 0.1
LANES = 128
HALO = 24
GUARD = 8
OWN = GUARD + HALO
FIELDS = 5
STEP = 16
ADV = 0.1 / 12.0
GRAV = 0.3 / 12.0
VISC = 0.004


def pairings(count):
    even = [i ^ 1 for i in range(count)]
    if count == 2:
        return [even]
    odd = [i if i in (0, count - 1) else ((i + 1) ^ 1) - 1 for i in range(count)]
    return [even, odd]


def roles(axis, count):
    place = lax.axis_index(axis)
    odd = lax.rem(place, 2)
    after_a = 1 - odd
    result = [(after_a, True)]
    if count > 2:
        after_b = odd
        exists = jnp.where(after_b == 1, place < count - 1, place > 0)
        result.append((after_b, exists))
    return result


def pack_kernel(counts, wet_ref, elev_ref, vel_ref, depth_ref, turb_ref, *outs):
    rows = elev_ref.shape[0]
    fields = [elev_ref[...], vel_ref[0], vel_ref[1], depth_ref[...], turb_ref[...]]
    refs = [elev_ref, vel_ref.at[0], vel_ref.at[1], depth_ref, turb_ref]
    wet = wet_ref[0, 0, 0].astype(jnp.float32)
    roles_x = roles("gx", counts[0])
    roles_y = roles("gy", counts[1])
    outs = list(outs)
    row_outs = [outs.pop(0) for _ in roles_x]
    side_outs = [outs.pop(0) for _ in roles_y]
    starts = [pl.multiple_of(after * (rows - HALO), 8) for after, _ in roles_x]
    for start, out in zip(starts, row_outs):
        for f, ref in enumerate(refs):
            out[HALO * f : HALO * (f + 1), :] = ref[pl.ds(start, HALO), :]
        out[HALO * FIELDS :, :] = jnp.full((LANES - HALO * FIELDS, LANES), wet, jnp.float32)
    lane = lax.broadcasted_iota(jnp.int32, (rows, LANES), 1)
    for (after, _), out in zip(roles_y, side_outs):
        packed = jnp.full((rows, LANES), wet, jnp.float32)
        for f in reversed(range(FIELDS)):
            moved = jnp.where(
                after == 1,
                pltpu.roll(fields[f], HALO * (f + 1), 1),
                pltpu.roll(fields[f], HALO * f, 1),
            )
            packed = jnp.where(lane < HALO * (f + 1), moved, packed)
        out[...] = packed
    for start in starts:
        for side in side_outs:
            outs.pop(0)[...] = side[pl.ds(start, HALO), :]


def shift_y(field, by):
    return pltpu.roll(field, (-by) % LANES, 1)


def main_kernel(
    counts, wet_ref, elev_ref, vel_ref, depth_ref, turb_ref, farm_ref, *rest
):
    rows = elev_ref.shape[0]
    rest = list(rest)
    nx, ny = counts
    roles_x = roles("gx", nx)
    roles_y = roles("gy", ny)
    row_in = [rest.pop(0) for _ in roles_x]
    left_in = rest.pop(0)
    right_in = rest.pop(0)
    corner_in = [(rest.pop(0), rest.pop(0)) for _ in roles_x]
    adj_ref, grad_ref, own_sum_ref, other_sum_ref, S = rest
    place_x = lax.axis_index("gx")
    place_y = lax.axis_index("gy")
    has_left = place_y > 0
    has_right = place_y < ny - 1
    wet = wet_ref[0, 0, 0].astype(jnp.float32)

    names = ["w", "T", "c", "d"]
    for k in range(6):
        names += [n + str(k) for n in ("h", "u", "v", "H", "F", "xu", "xv", "yu", "yv", "dm", "E", "rH")]
        names += [n + str(k) for n in ("lh", "lu", "lv", "uu", "uv")]
    names += ["acc", "oh", "ou", "ov"]
    at = {n: i for i, n in enumerate(names)}

    def lane_of(n):
        return lax.broadcasted_iota(jnp.int32, (n, LANES), 1)

    def put(start, n, centre, left, right, wet_centre, exists):
        lane = lane_of(n)
        in_left = lane < HALO
        in_right = lane >= LANES - HALO

        def windows(f, value):
            c = centre(f)
            if exists is not True:
                c = jnp.where(exists, c, value)
            ok_left = has_left if exists is True else jnp.logical_and(has_left, exists)
            ok_right = has_right if exists is True else jnp.logical_and(has_right, exists)
            from_left = jnp.where(ok_left, pltpu.roll(left, (-HALO * f) % LANES, 1), value)
            from_right = jnp.where(ok_right, pltpu.roll(right, (-HALO * (f + 1)) % LANES, 1), value)
            return (
                jnp.where(in_left, from_left, pltpu.roll(c, HALO, 1)),
                jnp.where(in_right, from_right, pltpu.roll(c, LANES - HALO, 1)),
            )

        hs = windows(0, 0.0)
        us = windows(1, 0.0)
        vs = windows(2, 0.0)
        ds = windows(3, 1.0)
        ts = windows(4, 0.0)
        wc = wet_centre
        ok_left = has_left
        ok_right = has_right
        if exists is not True:
            wc = jnp.where(exists, wc, 0.0)
            ok_left = jnp.logical_and(has_left, exists)
            ok_right = jnp.logical_and(has_right, exists)
        wl = jnp.where(ok_left, jnp.broadcast_to(left[:, LANES - 1 :], (n, LANES)), 0.0)
        wr = jnp.where(ok_right, jnp.broadcast_to(right[:, LANES - 1 :], (n, LANES)), 0.0)
        ws = (jnp.where(in_left, wl, wc), jnp.where(in_right, wr, wc))
        for t in range(2):
            def store(name, value):
                S[at[name], t, pl.ds(start, n), :] = value

            store("w", ws[t])
            store("T", ts[t])
            store("c", 0.5 * (BED_DRAG + ts[t]))
            store("d", ds[t])
            store("h0", hs[t])
            store("u0", us[t])
            store("v0", vs[t])
            height = ds[t] + hs[t]
            store("H0", height)
            store("F0", height * us[t])

    own = [elev_ref, vel_ref.at[0], vel_ref.at[1], depth_ref, turb_ref]
    put(OWN, rows, lambda f: own[f][...], left_in[...], right_in[...], wet, True)
    for (after, exists), rin, (cl, cr) in zip(roles_x, row_in, corner_in):
        start = pl.multiple_of(GUARD + after * (rows + HALO), 8)
        put(
            start,
            HALO,
            lambda f: rin[HALO * f : HALO * (f + 1), :],
            cl[...],
            cr[...],
            jnp.broadcast_to(rin[LANES - 1 :, :], (HALO, LANES)),
            exists,
        )

    def sweep(blocks, body):
        def step(i, carry):
            r0 = pl.multiple_of(OWN - 8 * blocks + i * STEP, 8)
            for t in range(2):
                body(
                    lambda name, s=0: S[at[name], t, pl.ds(r0 + s, STEP), :],
                    lambda name, value: S.__setitem__((at[name], t, pl.ds(r0, STEP), slice(None)), value),
                )
            return carry

        lax.fori_loop(0, (rows + 16 * blocks) // STEP, step, 0)

    def d_rows(L, name):
        return 8.0 * (L(name, 1) - L(name, -1)) - (L(name, 2) - L(name, -2))

    def d_cols(f):
        e = f - shift_y(f, -2)
        return 8.0 * shift_y(e, 1) - (shift_y(e, 2) + e)

    def velocity_terms(L, name, f):
        up1, um1, up2, um2 = L(name, 1), L(name, -1), L(name, 2), L(name, -2)
        dx = 8.0 * (up1 - um1) - (up2 - um2)
        yp2, ym2 = shift_y(f, 2), shift_y(f, -2)
        dy = 8.0 * shift_y(f - ym2, 1) - (yp2 - ym2)
        g = (up1 + um1) - 4.0 * f
        sg = shift_y(g + shift_y(g, -2), 1)
        far = (up2 + um2) + (yp2 + ym2)
        bi = far - 12.0 * f + 2.0 * (sg - 4.0 * g)
        return dx, dy, bi

    def tend(L, St, k, with_h):
        u, v, H = L("u%d" % k), L("v%d" % k), L("H%d" % k)
        xu, yu, bu = velocity_terms(L, "u%d" % k, u)
        xv, yv, bv = velocity_terms(L, "v%d" % k, v)
        h = L("h%d" % k)
        xh = d_rows(L, "h%d" % k)
        yh = d_cols(h)
        q2 = u * u + v * v + SPEED_EPS
        rH = 1.0 / H
        E = L("c") * (lax.rsqrt(q2) * rH)
        damp = E * q2
        for name, value in (("xu", xu), ("xv", xv), ("yu", yu), ("yv", yv), ("dm", damp), ("E", E), ("rH", rH)):
            St(name + str(k), value)
        ku = -ADV * (u * xu + v * yu) - GRAV * xh - damp * u - VISC * bu
        kv = -ADV * (u * xv + v * yv) - GRAV * yh - damp * v - VISC * bv
        if not with_h:
            return None, ku, kv
        kh = -ADV * (d_rows(L, "F%d" % k) + d_cols(H * v))
        return kh, ku, kv

    def keep_state(L, St, k, h, u, v):
        H = L("d") + h
        St("h%d" % k, h)
        St("u%d" % k, u)
        St("v%d" % k, v)
        St("H%d" % k, H)
        St("F%d" % k, H * u)

    hb = [-(-(22 - 2 * k) // 8) for k in range(6)]
    for n in range(2):
        s, a, b = 3 * n, 3 * n + 1, 3 * n + 2

        def first(L, St):
            w = L("w")
            ks = tend(L, St, s, True)
            keep_state(L, St, a, *[w * (L(x + str(s)) + k) for x, k in zip("huv", ks)])

        sweep(hb[s], first)

        def second(L, St):
            w = L("w")
            ks = tend(L, St, a, True)
            keep_state(
                L, St, b,
                *[w * (0.75 * L(x + str(s)) + 0.25 * (L(x + str(a)) + k)) for x, k in zip("huv", ks)],
            )

        sweep(hb[a], second)

        def third(L, St):
            w = L("w")
            ks = tend(L, St, b, n == 0)
            new = [
                None if k is None else w * (L(x + str(s)) * (1.0 / 3.0) + (2.0 / 3.0) * (L(x + str(b)) + k))
                for x, k in zip("huv", ks)
            ]
            if n == 0:
                keep_state(L, St, 3, *new)
                return
            u, v = new[1], new[2]
            q2 = u * u + v * v + SPEED_EPS
            q = jnp.sqrt(q2)
            St("acc", w * q2 * q)
            fac = (2.0 * w) * (L("T") * w * q)
            lu, lv = fac * u, fac * v
            ub = L("u5")
            St("lu5", lu)
            St("lv5", lv)
            St("uu5", ub * lu)
            St("uv5", ub * lv)

        sweep(hb[b], third)

    def pull(L, St, k, with_h):
        u, v, H = L("u%d" % k), L("v%d" % k), L("H%d" % k)
        lu, lv = L("lu%d" % k), L("lv%d" % k)
        nlu, nlv = "lu%d" % k, "lv%d" % k
        damp, E, rH = L("dm%d" % k), L("E%d" % k), L("rH%d" % k)
        xlu, _, blu = velocity_terms(L, nlu, lu)
        _, ylv, blv = velocity_terms(L, nlv, lv)
        r = lu * u + lv * v
        rd = r * damp
        rE = r * E
        ub = d_rows(L, "uu%d" % k) + d_cols(v * lu) - lu * L("xu%d" % k) - lv * L("xv%d" % k)
        vb = d_rows(L, "uv%d" % k) + d_cols(v * lv) - lu * L("yu%d" % k) - lv * L("yv%d" % k)
        hbar = GRAV * (xlu + ylv) + rd * rH
        if with_h:
            xlh = d_rows(L, "lh%d" % k)
            ylh = d_cols(L("lh%d" % k))
            ub = ub + H * xlh
            vb = vb + H * ylh
            hbar = hbar + ADV * (u * xlh + v * ylh)
        ub = ADV * ub - VISC * blu - (damp * lu + rE * u)
        vb = ADV * vb - VISC * blv - (damp * lv + rE * v)
        return hbar, ub, vb, rd

    drag = {k: [] for k in range(6)}

    def cot(L, name, k):
        return L(name + str(k))

    def keep_cot(L, St, k, lh, lu, lv):
        u = L("u%d" % k)
        St("lh%d" % k, lh)
        St("lu%d" % k, lu)
        St("lv%d" % k, lv)
        St("uu%d" % k, u * lu)
        St("uv%d" % k, u * lv)

    bb = [-(-(10 - 2 * k) // 8) for k in range(6)]
    for n in (1, 0):
        s, a, b = 3 * n, 3 * n + 1, 3 * n + 2
        first_pull = n == 1

        def from_b(L, St):
            w = L("w")
            hbar, ub, vb, rd = pull(L, St, b, not first_pull)
            St("acc", L("acc") - rd / (2.0 * L("c")))
            nh = hbar if first_pull else hbar + cot(L, "lh", b)
            quarter = 0.25 * w
            keep_cot(L, St, a, quarter * nh, quarter * (ub + cot(L, "lu", b)), quarter * (vb + cot(L, "lv", b)))

        sweep(bb[5 - b], from_b)

        def from_a(L, St):
            w = L("w")
            hbar, ub, vb, rd = pull(L, St, a, True)
            St("acc", L("acc") - rd / (2.0 * L("c")))
            keep_cot(
                L, St, s,
                w * (hbar + cot(L, "lh", a)), w * (ub + cot(L, "lu", a)), w * (vb + cot(L, "lv", a)),
            )

        sweep(bb[5 - a], from_a)

        def from_s(L, St):
            w = L("w")
            hbar, ub, vb, rd = pull(L, St, s, True)
            St("acc", L("acc") - rd / (2.0 * L("c")))
            new = []
            for x, value in (("lh", hbar), ("lu", ub), ("lv", vb)):
                total = value + cot(L, x, s) + 3.0 * cot(L, x, a)
                if not (first_pull and x == "lh"):
                    total = total + 0.5 * cot(L, x, b)
                new.append(total)
            if first_pull:
                scale = (2.0 / 3.0) * w
                keep_cot(L, St, 2, *[scale * x for x in new])
            else:
                for name, value in zip(("oh", "ou", "ov"), new):
                    St(name, value)

        sweep(bb[5 - s], from_s)

    def own_columns(name):
        lane = lane_of(rows)
        return jnp.where(
            lane < LANES // 2,
            pltpu.roll(S[at[name], 0, OWN : OWN + rows, :], LANES - HALO, 1),
            pltpu.roll(S[at[name], 1, OWN : OWN + rows, :], HALO, 1),
        )

    for i, name in enumerate(("oh", "ou", "ov")):
        adj_ref[i] = own_columns(name)
    grad = own_columns("acc")
    grad_ref[...] = grad
    matched = farm_ref[...] == place_x * ny + place_y
    scale = 1.0 / (rows * LANES)
    own_sum_ref[0] = jnp.sum(jnp.where(matched, grad, 0.0)) * scale
    other_sum_ref[0] = jnp.sum(jnp.where(matched, 0.0, grad)) * scale


def shards(elevation, velocity, depth, turbine, wet_tiles, farm):
    rows = elevation.shape[0]
    counts = (lax.axis_size("gx"), lax.axis_size("gy"))
    nx, ny = counts
    elev = elevation.reshape(rows, LANES)
    vel = velocity.reshape(2, rows, LANES)
    dep = depth.reshape(rows, LANES)
    turb = turbine.reshape(rows, LANES)
    farm_local = farm.reshape(rows, LANES)
    pairs_x = pairings(nx)
    pairs_y = pairings(ny)
    f32 = jnp.float32
    square = jax.ShapeDtypeStruct((LANES, LANES), f32)
    side = jax.ShapeDtypeStruct((rows, LANES), f32)
    corner = jax.ShapeDtypeStruct((HALO, LANES), f32)
    vmem = pl.BlockSpec(memory_space=pltpu.VMEM)
    smem = pl.BlockSpec(memory_space=pltpu.SMEM)
    shapes = [square] * len(pairs_x) + [side] * len(pairs_y) + [corner] * (len(pairs_x) * len(pairs_y))
    sent = pl.pallas_call(
        lambda *refs: pack_kernel(counts, *refs),
        out_shape=shapes,
        in_specs=[smem] + [vmem] * 4,
        out_specs=[vmem] * len(shapes),
        name="pack",
    )(wet_tiles, elev, vel, dep, turb)
    sent = list(sent)
    row_got = [lax.ppermute(sent.pop(0), "gx", list(enumerate(p))) for p in pairs_x]
    side_got = [lax.ppermute(sent.pop(0), "gy", list(enumerate(p))) for p in pairs_y]
    corner_got = [
        [
            lax.ppermute(
                sent.pop(0),
                ("gx", "gy"),
                [(i * ny + j, px[i] * ny + py[j]) for i in range(nx) for j in range(ny)],
            )
            for py in pairs_y
        ]
        for px in pairs_x
    ]

    def left_right(got):
        if len(got) == 1:
            return got[0], got[0]
        odd = lax.rem(lax.axis_index("gy"), 2) == 1
        return jnp.where(odd, got[0], got[1]), jnp.where(odd, got[1], got[0])

    left, right = left_right(side_got)
    corners = [c for got in corner_got for c in left_right(got)]
    n_in = 6 + len(row_got) + 2 + len(corners)
    planes = 4 + 6 * 17 + 4
    adjoint, grad, own_sum, other_sum = pl.pallas_call(
        lambda *refs: main_kernel(counts, *refs),
        out_shape=[
            jax.ShapeDtypeStruct((3, rows, LANES), f32),
            side,
            jax.ShapeDtypeStruct((1,), f32),
            jax.ShapeDtypeStruct((1,), f32),
        ],
        in_specs=[smem] + [vmem] * (n_in - 1),
        out_specs=[vmem, vmem, smem, smem],
        scratch_shapes=[pltpu.VMEM((planes, 2, rows + 2 * OWN, LANES), f32)],
        compiler_params=pltpu.CompilerParams(vmem_limit_bytes=40 * 1024 * 1024),
        name="adjoint",
    )(wet_tiles, elev, vel, dep, turb, farm_local, *row_got, left, right, *corners)
    passed = lax.ppermute(other_sum, "gx", [(i, (i + 1) % nx) for i in range(nx)])
    return (
        adjoint.reshape((3,) + elevation.shape),
        grad.reshape(elevation.shape),
        own_sum + passed,
    )


def solution(mesh):
    in_specs = (
        P("gx", None, "gy", None),
        P(None, "gx", None, "gy", None),
        P("gx", None, "gy", None),
        P("gx", None, "gy", None),
        P("gx", None, "gy"),
        P("gx", None, "gy", None),
    )
    out_specs = (P(None, "gx", None, "gy", None), P("gx", None, "gy", None), P(("gx", "gy")))
    return jax.shard_map(shards, mesh=mesh, in_specs=in_specs, out_specs=out_specs, check_vma=False)
```

```python
import jax
import jax.numpy as jnp
from jax import lax
from jax.experimental import pallas as pl
from jax.experimental.pallas import tpu as pltpu
from jax.sharding import PartitionSpec as P

SPEED_EPS = 0.01
BED_DRAG = 0.1
LANES = 128
HALO = 24
GUARD = 8
OWN = GUARD + HALO
FIELDS = 5
STEP = 16
UNROLL = 2
WIDE = LANES + 2 * HALO
ADV = 0.1 / 12.0
GRAV = 0.3 / 12.0
VISC = 0.004


def pairings(count):
    even = [i ^ 1 for i in range(count)]
    if count == 2:
        return [even]
    odd = [i if i in (0, count - 1) else ((i + 1) ^ 1) - 1 for i in range(count)]
    return [even, odd]


def roles(axis, count):
    place = lax.axis_index(axis)
    odd = lax.rem(place, 2)
    after_a = 1 - odd
    result = [(after_a, True)]
    if count > 2:
        after_b = odd
        exists = jnp.where(after_b == 1, place < count - 1, place > 0)
        result.append((after_b, exists))
    return result


def pack_kernel(counts, wet_ref, elev_ref, vel_ref, depth_ref, turb_ref, *outs):
    rows = elev_ref.shape[0]
    fields = [elev_ref[...], vel_ref[0], vel_ref[1], depth_ref[...], turb_ref[...]]
    refs = [elev_ref, vel_ref.at[0], vel_ref.at[1], depth_ref, turb_ref]
    wet = wet_ref[...].astype(jnp.float32)
    roles_x = roles("gx", counts[0])
    roles_y = roles("gy", counts[1])
    outs = list(outs)
    row_outs = [outs.pop(0) for _ in roles_x]
    side_outs = [outs.pop(0) for _ in roles_y]
    starts = [pl.multiple_of(after * (rows - HALO), 8) for after, _ in roles_x]
    for start, out in zip(starts, row_outs):
        for f, ref in enumerate(refs):
            out[HALO * f : HALO * (f + 1), :] = ref[pl.ds(start, HALO), :]
        out[HALO * FIELDS :, :] = jnp.broadcast_to(wet, (LANES - HALO * FIELDS, LANES))
    lane = lax.broadcasted_iota(jnp.int32, (rows, LANES), 1)
    for (after, _), out in zip(roles_y, side_outs):
        packed = jnp.broadcast_to(wet, (rows, LANES))
        for f in reversed(range(FIELDS)):
            moved = jnp.where(
                after == 1,
                pltpu.roll(fields[f], HALO * (f + 1), 1),
                pltpu.roll(fields[f], HALO * f, 1),
            )
            packed = jnp.where(lane < HALO * (f + 1), moved, packed)
        out[...] = packed
    for start in starts:
        for side in side_outs:
            outs.pop(0)[...] = side[pl.ds(start, HALO), :]


class Pair:
    def __init__(self, even, odd):
        self.even, self.odd = even, odd

    def map(self, function):
        return Pair(function(self.even), function(self.odd))

    def __add__(self, other):
        return both(self, other, lambda a, b: a + b)

    def __sub__(self, other):
        return both(self, other, lambda a, b: a - b)

    def __mul__(self, other):
        return both(self, other, lambda a, b: a * b)

    def __truediv__(self, other):
        return both(self, other, lambda a, b: a / b)

    def __rmul__(self, other):
        return self.map(lambda a: other * a)


def both(a, b, function):
    if isinstance(b, Pair):
        return Pair(function(a.even, b.even), function(a.odd, b.odd))
    return Pair(function(a.even, b), function(a.odd, b))


def after(x):
    return pltpu.roll(x, LANES - 1, 1)


def before(x):
    return pltpu.roll(x, 1, 1)


def d_cols(f):
    ea, eb, oa, ob = after(f.even), before(f.even), after(f.odd), before(f.odd)
    slope = Pair(
        8.0 * (f.odd - ob) - (ea - eb),
        8.0 * (ea - f.even) - (oa - ob),
    )
    return slope, Pair(ea + eb, oa + ob)


def combine(p1, m1, p2, m2):
    return Pair(
        (p1.odd + after(p2.even)) + before(m1.odd + m2.even),
        (m1.even + after(p1.even + p2.odd)) + before(m2.odd),
    )


def thirds(x):
    one = x.astype(jnp.bfloat16)
    rest = x - one.astype(jnp.float32)
    two = rest.astype(jnp.bfloat16)
    three = (rest - two.astype(jnp.float32)).astype(jnp.bfloat16)
    return one, two, three


def pick(x, chosen):
    parts = [jnp.dot(part, chosen, preferred_element_type=jnp.float32) for part in thirds(x)]
    return (parts[0] + parts[1]) + parts[2]


def main_kernel(counts, wet_ref, elev_ref, vel_ref, depth_ref, turb_ref, farm_ref, *rest):
    rows = elev_ref.shape[0]
    rest = list(rest)
    nx, ny = counts
    roles_x = roles("gx", nx)
    row_in = [rest.pop(0) for _ in roles_x]
    sides = 1 if ny == 2 else 2
    side_in = [rest.pop(0) for _ in range(sides)]
    corner_in = [[rest.pop(0) for _ in range(sides)] for _ in roles_x]
    adj_ref, grad_ref, own_sum_ref, other_sum_ref, S = rest
    place_x = lax.axis_index("gx")
    place_y = lax.axis_index("gy")
    has_left = place_y > 0
    has_right = place_y < ny - 1
    wet = wet_ref[...].astype(jnp.float32)

    names = ["w", "T", "c", "d"]
    for k in range(6):
        names += [n + str(k) for n in ("h", "u", "v", "H", "F", "xu", "xv", "yu", "yv", "dm", "E", "rH")]
        names += [n + str(k) for n in ("lh", "lu", "lv", "uu", "uv")]
    names += ["acc", "oh", "ou", "ov"]
    at = {n: i for i, n in enumerate(names)}

    def column_at(shape, dim):
        place = lax.broadcasted_iota(jnp.int32, shape, dim)
        return 2 * lax.rem(place, LANES) + lax.div(place, LANES)

    def spread(f):
        shape = (LANES, 2 * LANES)
        target = column_at(shape, 1)
        source = lax.broadcasted_iota(jnp.int32, shape, 0)
        blocks = [source + HALO == target]
        edge = source - HALO * f
        inside = jnp.logical_and(edge >= 0, edge < HALO)
        if sides == 1:
            offset = jnp.where(has_left, 0, LANES + HALO)
            blocks.append(jnp.logical_and(inside, edge + offset == target))
        else:
            hit_left = jnp.logical_and(inside, edge == target)
            hit_right = jnp.logical_and(inside, edge + (LANES + HALO) == target)
            blocks.append(jnp.logical_and(hit_left, has_left))
            blocks.append(jnp.logical_and(hit_right, has_right))
        return jnp.concatenate(
            [jnp.where(b, 1.0, 0.0).astype(jnp.bfloat16) for b in blocks], axis=0
        )

    chosen = [spread(f) for f in range(FIELDS)]

    def put(start, n, centre, edges, wet_centre, exists):
        column = column_at((n, 2 * LANES), 1)
        in_left = column < HALO
        in_right = column >= LANES + HALO
        known = jnp.logical_and(
            jnp.logical_or(jnp.logical_not(in_left), has_left),
            jnp.logical_or(jnp.logical_not(in_right), has_right),
        )
        known = jnp.logical_and(known, column < WIDE)
        if exists is not True:
            known = jnp.logical_and(known, exists)
        values = [
            jnp.where(known, pick(jnp.concatenate([centre(f)] + edges, axis=1), chosen[f]), 1.0 if f == 3 else 0.0)
            for f in range(FIELDS)
        ]
        wet_left = jnp.broadcast_to(edges[0][:, LANES - 1 :], (n, 2 * LANES))
        wet_right = jnp.broadcast_to(edges[-1][:, LANES - 1 :], (n, 2 * LANES))
        w = jnp.where(in_left, wet_left, jnp.where(in_right, wet_right, wet_centre))
        w = jnp.where(known, w, 0.0)
        h, u, v, d, turb = values
        height = d + h
        planes = (
            ("w", w), ("T", turb), ("c", 0.5 * (BED_DRAG + turb)), ("d", d),
            ("h0", h), ("u0", u), ("v0", v), ("H0", height), ("F0", height * u),
        )
        for name, value in planes:
            for t in range(2):
                S[at[name], t, pl.ds(start, n), :] = value[:, LANES * t : LANES * (t + 1)]

    own = [elev_ref, vel_ref.at[0], vel_ref.at[1], depth_ref, turb_ref]
    put(
        OWN, rows, lambda f: own[f][...], [x[...] for x in side_in],
        jnp.broadcast_to(wet, (rows, 2 * LANES)), True,
    )
    for (partner_after, exists), rin, corners in zip(roles_x, row_in, corner_in):
        put(
            pl.multiple_of(GUARD + partner_after * (rows + HALO), 8),
            HALO,
            lambda f: rin[HALO * f : HALO * (f + 1), :],
            [x[...] for x in corners],
            jnp.broadcast_to(rin[LANES - 1 :, :1], (HALO, 2 * LANES)),
            exists,
        )

    def sweep(blocks, body):
        count = (rows + 16 * blocks) // STEP

        def chunk(r0):
            def load(name, s=0):
                return Pair(*[S[at[name], t, pl.ds(r0 + s, STEP), :] for t in range(2)])

            def store(name, value):
                S[at[name], 0, pl.ds(r0, STEP), :] = value.even
                S[at[name], 1, pl.ds(r0, STEP), :] = value.odd

            body(load, store)

        def step(i, carry):
            for k in range(UNROLL):
                chunk(pl.multiple_of(OWN - 8 * blocks + (i * UNROLL + k) * STEP, 8))
            return carry

        lax.fori_loop(0, count // UNROLL, step, 0)
        for k in range(count // UNROLL * UNROLL, count):
            chunk(OWN - 8 * blocks + k * STEP)

    def d_rows(L, name):
        p1, m1, p2, m2 = L(name, 1), L(name, -1), L(name, 2), L(name, -2)
        return 8.0 * (p1 - m1) - (p2 - m2), p1 + m1, p2 + m2

    def tend(L, St, k, with_h):
        u, v, H, h = L("u%d" % k), L("v%d" % k), L("H%d" % k), L("h%d" % k)
        xu, su, tu = d_rows(L, "u%d" % k)
        xv, sv, tv = d_rows(L, "v%d" % k)
        yu, ru = d_cols(u)
        yv, rv = d_cols(v)
        gu = su - 4.0 * u
        gv = sv - 4.0 * v
        near_u = Pair(gu.odd + before(gu.odd), gu.even + after(gu.even))
        bu = ((tu + ru) - 12.0 * u) + 2.0 * (near_u - 4.0 * gu)
        bv = ((tv + rv) - 12.0 * v) - 8.0 * gv
        far = 8.0 * h
        near_v = (2.0 * VISC / GRAV) * gv
        yh = combine(far + near_v, near_v - far, -1.0 * h, h)
        xh = d_rows(L, "h%d" % k)[0]
        q2 = (u * u + v * v) + SPEED_EPS
        rH = H.map(lambda x: 1.0 / x)
        E = L("c") * (q2.map(lax.rsqrt) * rH)
        damp = E * q2
        for name, value in (("xu", xu), ("xv", xv), ("yu", yu), ("yv", yv), ("dm", damp), ("E", E), ("rH", rH)):
            St(name + str(k), value)
        ku = (-ADV) * (u * xu + v * yu) - GRAV * xh - damp * u - VISC * bu
        kv = (-ADV) * (u * xv + v * yv) - GRAV * yh - damp * v - VISC * bv
        if not with_h:
            return None, ku, kv
        kh = (-ADV) * (d_rows(L, "F%d" % k)[0] + d_cols(H * v)[0])
        return kh, ku, kv

    def keep_state(L, St, k, h, u, v):
        H = L("d") + h
        St("h%d" % k, h)
        St("u%d" % k, u)
        St("v%d" % k, v)
        St("H%d" % k, H)
        St("F%d" % k, H * u)

    hb = [-(-(22 - 2 * k) // 8) for k in range(6)]
    for n in range(2):
        s, a, b = 3 * n, 3 * n + 1, 3 * n + 2

        def first(L, St):
            w = L("w")
            ks = tend(L, St, s, True)
            keep_state(L, St, a, *[w * (L(x + str(s)) + k) for x, k in zip("huv", ks)])

        sweep(hb[s], first)

        def second(L, St):
            w = L("w")
            ks = tend(L, St, a, True)
            keep_state(
                L, St, b,
                *[w * (0.75 * L(x + str(s)) + 0.25 * (L(x + str(a)) + k)) for x, k in zip("huv", ks)],
            )

        sweep(hb[a], second)

        def third(L, St):
            w = L("w")
            ks = tend(L, St, b, n == 0)
            new = [
                None if k is None else w * ((1.0 / 3.0) * L(x + str(s)) + (2.0 / 3.0) * (L(x + str(b)) + k))
                for x, k in zip("huv", ks)
            ]
            if n == 0:
                keep_state(L, St, 3, *new)
                return
            u, v = new[1], new[2]
            q2 = (u * u + v * v) + SPEED_EPS
            q = q2.map(jnp.sqrt)
            St("acc", w * q2 * q)
            fac = (2.0 * w) * (L("T") * w * q)
            lu, lv = fac * u, fac * v
            ub = L("u5")
            St("lu5", lu)
            St("lv5", lv)
            St("uu5", ub * lu)
            St("uv5", ub * lv)

        sweep(hb[b], third)

    def pull(L, k, with_h):
        u, v, H = L("u%d" % k), L("v%d" % k), L("H%d" % k)
        lu, lv = L("lu%d" % k), L("lv%d" % k)
        damp, E, rH = L("dm%d" % k), L("E%d" % k), L("rH%d" % k)
        visc = VISC / ADV
        xlu, su, tu = d_rows(L, "lu%d" % k)
        _, sv, tv = d_rows(L, "lv%d" % k)
        ylv, rv = d_cols(lv)
        gu = su - 4.0 * lu
        gv = sv - 4.0 * lv
        vl = v * lu
        vl8, near, lu_s = 8.0 * vl, (2.0 * visc) * gu, visc * lu
        ub = combine(vl8 - near, -1.0 * (vl8 + near), -1.0 * (vl + lu_s), vl - lu_s)
        ub = ub - visc * ((tu - 12.0 * lu) - 8.0 * gu)
        vl = v * lv
        vl8, near = 8.0 * vl, (2.0 * visc) * gv
        vb = combine(vl8 - near, -1.0 * (vl8 + near), -1.0 * vl, vl)
        vb = vb - visc * (((tv + rv) - 12.0 * lv) - 8.0 * gv)
        ub = ub + d_rows(L, "uu%d" % k)[0] - lu * L("xu%d" % k) - lv * L("xv%d" % k)
        vb = vb + d_rows(L, "uv%d" % k)[0] - lu * L("yu%d" % k) - lv * L("yv%d" % k)
        r = lu * u + lv * v
        rd = r * damp
        rE = r * E
        hbar = GRAV * (xlu + ylv) + rd * rH
        if with_h:
            xlh = d_rows(L, "lh%d" % k)[0]
            ylh = d_cols(L("lh%d" % k))[0]
            ub = ub + H * xlh
            vb = vb + H * ylh
            hbar = hbar + ADV * (u * xlh + v * ylh)
        ub = ADV * ub - (damp * lu + rE * u)
        vb = ADV * vb - (damp * lv + rE * v)
        return hbar, ub, vb, rd

    def keep_cot(L, St, k, lh, lu, lv):
        u = L("u%d" % k)
        St("lh%d" % k, lh)
        St("lu%d" % k, lu)
        St("lv%d" % k, lv)
        St("uu%d" % k, u * lu)
        St("uv%d" % k, u * lv)

    def add_drag(L, St, rd):
        St("acc", L("acc") - rd / (2.0 * L("c")))

    bb = [-(-(10 - 2 * k) // 8) for k in range(6)]
    for n in (1, 0):
        s, a, b = 3 * n, 3 * n + 1, 3 * n + 2
        top = n == 1

        def from_b(L, St):
            hbar, ub, vb, rd = pull(L, b, not top)
            add_drag(L, St, rd)
            quarter = 0.25 * L("w")
            new = [hbar if top else hbar + L("lh%d" % b), ub + L("lu%d" % b), vb + L("lv%d" % b)]
            keep_cot(L, St, a, *[quarter * x for x in new])

        sweep(bb[5 - b], from_b)

        def from_a(L, St):
            w = L("w")
            hbar, ub, vb, rd = pull(L, a, True)
            add_drag(L, St, rd)
            keep_cot(L, St, s, *[w * (x + L(y + str(a))) for x, y in zip((hbar, ub, vb), ("lh", "lu", "lv"))])

        sweep(bb[5 - a], from_a)

        def from_s(L, St):
            hbar, ub, vb, rd = pull(L, s, True)
            add_drag(L, St, rd)
            new = []
            for x, value in (("lh", hbar), ("lu", ub), ("lv", vb)):
                total = value + L(x + str(s)) + 3.0 * L(x + str(a))
                if not (top and x == "lh"):
                    total = total + 0.5 * L(x + str(b))
                new.append(total)
            if top:
                scale = (2.0 / 3.0) * L("w")
                keep_cot(L, St, 2, *[scale * x for x in new])
            else:
                for name, value in zip(("oh", "ou", "ov"), new):
                    St(name, value)

        sweep(bb[5 - s], from_s)

    shape = (2 * LANES, LANES)
    gather = column_at(shape, 0) == lax.broadcasted_iota(jnp.int32, shape, 1) + HALO
    gather = jnp.where(gather, 1.0, 0.0).astype(jnp.bfloat16)

    lane = lax.broadcasted_iota(jnp.int32, (rows, LANES), 1)
    in_tile = jnp.logical_and(lane >= HALO // 2, lane < (HALO + LANES) // 2)

    def own_columns(name):
        planes = [jnp.where(in_tile, S[at[name], t, OWN : OWN + rows, :], 0.0) for t in range(2)]
        return pick(jnp.concatenate(planes, axis=1), gather)

    for i, name in enumerate(("oh", "ou", "ov")):
        adj_ref[i] = own_columns(name)
    grad = own_columns("acc")
    grad_ref[...] = grad
    matched = farm_ref[...] == place_x * ny + place_y
    scale = 1.0 / (rows * LANES)
    own_sum_ref[0] = jnp.sum(jnp.where(matched, grad, 0.0)) * scale
    other_sum_ref[0] = jnp.sum(jnp.where(matched, 0.0, grad)) * scale


def shards(elevation, velocity, depth, turbine, wet_tiles, farm):
    rows = elevation.shape[0]
    counts = (lax.axis_size("gx"), lax.axis_size("gy"))
    nx, ny = counts
    wet = wet_tiles.reshape(1, 1)
    elev = elevation.reshape(rows, LANES)
    vel = velocity.reshape(2, rows, LANES)
    dep = depth.reshape(rows, LANES)
    turb = turbine.reshape(rows, LANES)
    farm_local = farm.reshape(rows, LANES)
    pairs_x = pairings(nx)
    pairs_y = pairings(ny)
    f32 = jnp.float32
    square = jax.ShapeDtypeStruct((LANES, LANES), f32)
    side = jax.ShapeDtypeStruct((rows, LANES), f32)
    corner = jax.ShapeDtypeStruct((HALO, LANES), f32)
    vmem = pl.BlockSpec(memory_space=pltpu.VMEM)
    smem = pl.BlockSpec(memory_space=pltpu.SMEM)
    shapes = [square] * len(pairs_x) + [side] * len(pairs_y) + [corner] * (len(pairs_x) * len(pairs_y))
    sent = pl.pallas_call(
        lambda *refs: pack_kernel(counts, *refs),
        out_shape=shapes,
        in_specs=[vmem] * 5,
        out_specs=[vmem] * len(shapes),
        name="pack",
    )(wet, elev, vel, dep, turb)
    sent = list(sent)
    row_got = [lax.ppermute(sent.pop(0), "gx", list(enumerate(p))) for p in pairs_x]
    side_got = [lax.ppermute(sent.pop(0), "gy", list(enumerate(p))) for p in pairs_y]
    corner_got = [
        [
            lax.ppermute(
                sent.pop(0),
                ("gx", "gy"),
                [(i * ny + j, px[i] * ny + py[j]) for i in range(nx) for j in range(ny)],
            )
            for py in pairs_y
        ]
        for px in pairs_x
    ]

    def left_right(got):
        if len(got) == 1:
            return got
        odd = lax.rem(lax.axis_index("gy"), 2) == 1
        return [jnp.where(odd, got[0], got[1]), jnp.where(odd, got[1], got[0])]

    edges = left_right(side_got)
    corners = [c for got in corner_got for c in left_right(got)]
    n_in = 6 + len(row_got) + len(edges) + len(corners)
    planes = 4 + 6 * 17 + 4
    adjoint, grad, own_sum, other_sum = pl.pallas_call(
        lambda *refs: main_kernel(counts, *refs),
        out_shape=[
            jax.ShapeDtypeStruct((3, rows, LANES), f32),
            side,
            jax.ShapeDtypeStruct((1,), f32),
            jax.ShapeDtypeStruct((1,), f32),
        ],
        in_specs=[vmem] * n_in,
        out_specs=[vmem, vmem, smem, smem],
        scratch_shapes=[pltpu.VMEM((planes, 2, rows + 2 * OWN, LANES), f32)],
        compiler_params=pltpu.CompilerParams(vmem_limit_bytes=40 * 1024 * 1024),
        name="adjoint",
    )(wet, elev, vel, dep, turb, farm_local, *row_got, *edges, *corners)
    passed = lax.ppermute(other_sum, "gx", [(i, (i + 1) % nx) for i in range(nx)])
    return (
        adjoint.reshape((3,) + elevation.shape),
        grad.reshape(elevation.shape),
        own_sum + passed,
    )


def solution(mesh):
    in_specs = (
        P("gx", None, "gy", None),
        P(None, "gx", None, "gy", None),
        P("gx", None, "gy", None),
        P("gx", None, "gy", None),
        P("gx", None, "gy"),
        P("gx", None, "gy", None),
    )
    out_specs = (P(None, "gx", None, "gy", None), P("gx", None, "gy", None), P(("gx", "gy")))
    return jax.shard_map(shards, mesh=mesh, in_specs=in_specs, out_specs=out_specs, check_vma=False)
```

```python
import jax
import jax.numpy as jnp
from jax import lax
from jax.experimental import pallas as pl
from jax.experimental.pallas import tpu as pltpu
from jax.sharding import PartitionSpec as P

SPEED_EPS = 0.01
BED_DRAG = 0.1
LANES = 128
HALO = 24
GUARD = 8
OWN = GUARD + HALO
FIELDS = 5
STEP = 16
WIDE = LANES + 2 * HALO
ADV = 0.1 / 12.0
GRAV = 0.3 / 12.0
VISC = 0.004


def pairings(count):
    even = [i ^ 1 for i in range(count)]
    if count == 2:
        return [even]
    odd = [i if i in (0, count - 1) else ((i + 1) ^ 1) - 1 for i in range(count)]
    return [even, odd]


def roles(axis, count):
    place = lax.axis_index(axis)
    odd = lax.rem(place, 2)
    after_a = 1 - odd
    result = [(after_a, True)]
    if count > 2:
        after_b = odd
        exists = jnp.where(after_b == 1, place < count - 1, place > 0)
        result.append((after_b, exists))
    return result


def pack_kernel(counts, wet_ref, elev_ref, vel_ref, depth_ref, turb_ref, farm_ref, *outs):
    rows = elev_ref.shape[0]
    fields = [elev_ref[...], vel_ref[0], vel_ref[1], depth_ref[...], turb_ref[...]]
    refs = [elev_ref, vel_ref.at[0], vel_ref.at[1], depth_ref, turb_ref]
    wet = wet_ref[0].astype(jnp.float32)
    roles_x = roles("gx", counts[0])
    roles_y = roles("gy", counts[1])
    outs = list(outs)
    outs.pop()[...] = jnp.broadcast_to(wet, (8, LANES))
    row_outs = [outs.pop(0) for _ in roles_x]
    side_outs = [outs.pop(0) for _ in roles_y]
    starts = [pl.multiple_of(after * (rows - HALO), 8) for after, _ in roles_x]
    for start, out in zip(starts, row_outs):
        for f, ref in enumerate(refs):
            out[HALO * f : HALO * (f + 1), :] = ref[pl.ds(start, HALO), :]
        out[HALO * FIELDS :, :] = jnp.broadcast_to(wet, (LANES - HALO * FIELDS, LANES))
    lane = lax.broadcasted_iota(jnp.int32, (rows, LANES), 1)
    for (after, _), out in zip(roles_y, side_outs):
        packed = jnp.broadcast_to(wet, (rows, LANES))
        for f in reversed(range(FIELDS)):
            moved = jnp.where(
                after == 1,
                pltpu.roll(fields[f], HALO * (f + 1), 1),
                pltpu.roll(fields[f], HALO * f, 1),
            )
            packed = jnp.where(lane < HALO * (f + 1), moved, packed)
        out[...] = packed
    for start in starts:
        for side in side_outs:
            outs.pop(0)[...] = side[pl.ds(start, HALO), :]


class Pair:
    def __init__(self, even, odd):
        self.even, self.odd = even, odd

    def map(self, function):
        return Pair(function(self.even), function(self.odd))

    def __add__(self, other):
        return both(self, other, lambda a, b: a + b)

    def __sub__(self, other):
        return both(self, other, lambda a, b: a - b)

    def __mul__(self, other):
        return both(self, other, lambda a, b: a * b)

    def __truediv__(self, other):
        return both(self, other, lambda a, b: a / b)

    def __rmul__(self, other):
        return self.map(lambda a: other * a)


def both(a, b, function):
    if isinstance(b, Pair):
        return Pair(function(a.even, b.even), function(a.odd, b.odd))
    return Pair(function(a.even, b), function(a.odd, b))


def after(x):
    return pltpu.roll(x, LANES - 1, 1)


def before(x):
    return pltpu.roll(x, 1, 1)


def d_cols(f):
    ea, eb, oa, ob = after(f.even), before(f.even), after(f.odd), before(f.odd)
    slope = Pair(
        8.0 * (f.odd - ob) - (ea - eb),
        8.0 * (ea - f.even) - (oa - ob),
    )
    return slope, Pair(ea + eb, oa + ob)


def combine(p1, m1, p2, m2):
    return Pair(
        (p1.odd + after(p2.even)) + before(m1.odd + m2.even),
        (m1.even + after(p1.even + p2.odd)) + before(m2.odd),
    )


def thirds(x):
    one = x.astype(jnp.bfloat16)
    rest = x - one.astype(jnp.float32)
    two = rest.astype(jnp.bfloat16)
    three = (rest - two.astype(jnp.float32)).astype(jnp.bfloat16)
    return one, two, three


def pick(x, chosen):
    parts = [jnp.dot(part, chosen, preferred_element_type=jnp.float32) for part in thirds(x)]
    return (parts[0] + parts[1]) + parts[2]


def main_kernel(counts, wet_ref, elev_ref, vel_ref, depth_ref, turb_ref, farm_ref, *rest):
    rows = elev_ref.shape[0]
    rest = list(rest)
    nx, ny = counts
    roles_x = roles("gx", nx)
    row_in = [rest.pop(0) for _ in roles_x]
    sides = 1 if ny == 2 else 2
    side_in = [rest.pop(0) for _ in range(sides)]
    corner_in = [[rest.pop(0) for _ in range(sides)] for _ in roles_x]
    adj_ref, grad_ref, own_sum_ref, other_sum_ref, S, farm_here, farm_sem = rest
    farm_copy = pltpu.make_async_copy(farm_ref, farm_here, farm_sem)
    farm_copy.start()
    place_x = lax.axis_index("gx")
    place_y = lax.axis_index("gy")
    has_left = place_y > 0
    has_right = place_y < ny - 1
    wet = wet_ref[:1, :1]

    names = ["w", "T", "c", "d"]
    for k in range(6):
        names += [n + str(k) for n in ("h", "u", "v", "H", "F", "xu", "xv", "yu", "yv", "dm", "E", "rH")]
        names += [n + str(k) for n in ("lh", "lu", "lv", "uu", "uv")]
    names += ["acc", "oh", "ou", "ov"]
    at = {n: i for i, n in enumerate(names)}

    def column_at(shape, dim):
        place = lax.broadcasted_iota(jnp.int32, shape, dim)
        return 2 * lax.rem(place, LANES) + lax.div(place, LANES)

    def spread(f):
        shape = (LANES, 2 * LANES)
        target = column_at(shape, 1)
        source = lax.broadcasted_iota(jnp.int32, shape, 0)
        blocks = [source + HALO == target]
        edge = source - HALO * f
        inside = jnp.logical_and(edge >= 0, edge < HALO)
        if sides == 1:
            offset = jnp.where(has_left, 0, LANES + HALO)
            blocks.append(jnp.logical_and(inside, edge + offset == target))
        else:
            hit_left = jnp.logical_and(inside, edge == target)
            hit_right = jnp.logical_and(inside, edge + (LANES + HALO) == target)
            blocks.append(jnp.logical_and(hit_left, has_left))
            blocks.append(jnp.logical_and(hit_right, has_right))
        return jnp.concatenate(
            [jnp.where(b, 1.0, 0.0).astype(jnp.bfloat16) for b in blocks], axis=0
        )

    chosen = [spread(f) for f in range(FIELDS)]

    def put(start, n, centre, edges, wet_centre, exists):
        column = column_at((n, 2 * LANES), 1)
        in_left = column < HALO
        in_right = column >= LANES + HALO
        known = jnp.logical_and(
            jnp.logical_or(jnp.logical_not(in_left), has_left),
            jnp.logical_or(jnp.logical_not(in_right), has_right),
        )
        known = jnp.logical_and(known, column < WIDE)
        if exists is not True:
            known = jnp.logical_and(known, exists)
        values = [
            jnp.where(known, pick(jnp.concatenate([centre(f)] + edges, axis=1), chosen[f]), 1.0 if f == 3 else 0.0)
            for f in range(FIELDS)
        ]
        wet_left = jnp.broadcast_to(edges[0][:, LANES - 1 :], (n, 2 * LANES))
        wet_right = jnp.broadcast_to(edges[-1][:, LANES - 1 :], (n, 2 * LANES))
        w = jnp.where(in_left, wet_left, jnp.where(in_right, wet_right, wet_centre))
        w = jnp.where(known, w, 0.0)
        h, u, v, d, turb = values
        height = d + h
        planes = (
            ("w", w), ("T", turb), ("c", 0.5 * (BED_DRAG + turb)), ("d", d),
            ("h0", h), ("u0", u), ("v0", v), ("H0", height), ("F0", height * u),
        )
        for name, value in planes:
            for t in range(2):
                S[at[name], t, pl.ds(start, n), :] = value[:, LANES * t : LANES * (t + 1)]

    own = [elev_ref, vel_ref.at[0], vel_ref.at[1], depth_ref, turb_ref]
    put(
        OWN, rows, lambda f: own[f][...], [x[...] for x in side_in],
        jnp.broadcast_to(wet, (rows, 2 * LANES)), True,
    )
    for (partner_after, exists), rin, corners in zip(roles_x, row_in, corner_in):
        put(
            pl.multiple_of(GUARD + partner_after * (rows + HALO), 8),
            HALO,
            lambda f: rin[HALO * f : HALO * (f + 1), :],
            [x[...] for x in corners],
            jnp.broadcast_to(rin[LANES - 1 :, :1], (HALO, 2 * LANES)),
            exists,
        )

    def sweep(blocks, body):
        count = (rows + 16 * blocks) // STEP

        def chunk(r0):
            def load(name, s=0):
                return Pair(*[S[at[name], t, pl.ds(r0 + s, STEP), :] for t in range(2)])

            def store(name, value):
                S[at[name], 0, pl.ds(r0, STEP), :] = value.even
                S[at[name], 1, pl.ds(r0, STEP), :] = value.odd

            body(load, store)

        for k in range(count):
            chunk(OWN - 8 * blocks + k * STEP)

    def d_rows(L, name):
        p1, m1, p2, m2 = L(name, 1), L(name, -1), L(name, 2), L(name, -2)
        return 8.0 * (p1 - m1) - (p2 - m2), p1 + m1, p2 + m2

    def tend(L, St, k, with_h):
        u, v, H, h = L("u%d" % k), L("v%d" % k), L("H%d" % k), L("h%d" % k)
        xu, su, tu = d_rows(L, "u%d" % k)
        xv, sv, tv = d_rows(L, "v%d" % k)
        yu, ru = d_cols(u)
        yv, rv = d_cols(v)
        gu = su - 4.0 * u
        gv = sv - 4.0 * v
        near_u = Pair(gu.odd + before(gu.odd), gu.even + after(gu.even))
        bu = ((tu + ru) - 12.0 * u) + 2.0 * (near_u - 4.0 * gu)
        bv = ((tv + rv) - 12.0 * v) - 8.0 * gv
        far = 8.0 * h
        near_v = (2.0 * VISC / GRAV) * gv
        yh = combine(far + near_v, near_v - far, -1.0 * h, h)
        xh = d_rows(L, "h%d" % k)[0]
        q2 = (u * u + v * v) + SPEED_EPS
        rH = H.map(lambda x: 1.0 / x)
        E = L("c") * (q2.map(lax.rsqrt) * rH)
        damp = E * q2
        for name, value in (("xu", xu), ("xv", xv), ("yu", yu), ("yv", yv), ("dm", damp), ("E", E), ("rH", rH)):
            St(name + str(k), value)
        ku = (-ADV) * (u * xu + v * yu) - GRAV * xh - damp * u - VISC * bu
        kv = (-ADV) * (u * xv + v * yv) - GRAV * yh - damp * v - VISC * bv
        if not with_h:
            return None, ku, kv
        kh = (-ADV) * (d_rows(L, "F%d" % k)[0] + d_cols(H * v)[0])
        return kh, ku, kv

    def keep_state(L, St, k, h, u, v):
        H = L("d") + h
        St("h%d" % k, h)
        St("u%d" % k, u)
        St("v%d" % k, v)
        St("H%d" % k, H)
        St("F%d" % k, H * u)

    hb = [-(-(22 - 2 * k) // 8) for k in range(6)]
    for n in range(2):
        s, a, b = 3 * n, 3 * n + 1, 3 * n + 2

        def first(L, St):
            w = L("w")
            ks = tend(L, St, s, True)
            keep_state(L, St, a, *[w * (L(x + str(s)) + k) for x, k in zip("huv", ks)])

        sweep(hb[s], first)

        def second(L, St):
            w = L("w")
            ks = tend(L, St, a, True)
            keep_state(
                L, St, b,
                *[w * (0.75 * L(x + str(s)) + 0.25 * (L(x + str(a)) + k)) for x, k in zip("huv", ks)],
            )

        sweep(hb[a], second)

        def third(L, St):
            w = L("w")
            ks = tend(L, St, b, n == 0)
            new = [
                None if k is None else w * ((1.0 / 3.0) * L(x + str(s)) + (2.0 / 3.0) * (L(x + str(b)) + k))
                for x, k in zip("huv", ks)
            ]
            if n == 0:
                keep_state(L, St, 3, *new)
                return
            u, v = new[1], new[2]
            q2 = (u * u + v * v) + SPEED_EPS
            q = q2.map(jnp.sqrt)
            St("acc", w * q2 * q)
            fac = (2.0 * w) * (L("T") * w * q)
            lu, lv = fac * u, fac * v
            ub = L("u5")
            St("lu5", lu)
            St("lv5", lv)
            St("uu5", ub * lu)
            St("uv5", ub * lv)

        sweep(hb[b], third)

    def pull(L, k, with_h):
        u, v, H = L("u%d" % k), L("v%d" % k), L("H%d" % k)
        lu, lv = L("lu%d" % k), L("lv%d" % k)
        damp, E, rH = L("dm%d" % k), L("E%d" % k), L("rH%d" % k)
        visc = VISC / ADV
        xlu, su, tu = d_rows(L, "lu%d" % k)
        _, sv, tv = d_rows(L, "lv%d" % k)
        ylv, rv = d_cols(lv)
        gu = su - 4.0 * lu
        gv = sv - 4.0 * lv
        vl = v * lu
        vl8, near, lu_s = 8.0 * vl, (2.0 * visc) * gu, visc * lu
        ub = combine(vl8 - near, -1.0 * (vl8 + near), -1.0 * (vl + lu_s), vl - lu_s)
        ub = ub - visc * ((tu - 12.0 * lu) - 8.0 * gu)
        vl = v * lv
        vl8, near = 8.0 * vl, (2.0 * visc) * gv
        vb = combine(vl8 - near, -1.0 * (vl8 + near), -1.0 * vl, vl)
        vb = vb - visc * (((tv + rv) - 12.0 * lv) - 8.0 * gv)
        ub = ub + d_rows(L, "uu%d" % k)[0] - lu * L("xu%d" % k) - lv * L("xv%d" % k)
        vb = vb + d_rows(L, "uv%d" % k)[0] - lu * L("yu%d" % k) - lv * L("yv%d" % k)
        r = lu * u + lv * v
        rd = r * damp
        rE = r * E
        hbar = GRAV * (xlu + ylv) + rd * rH
        if with_h:
            xlh = d_rows(L, "lh%d" % k)[0]
            ylh = d_cols(L("lh%d" % k))[0]
            ub = ub + H * xlh
            vb = vb + H * ylh
            hbar = hbar + ADV * (u * xlh + v * ylh)
        ub = ADV * ub - (damp * lu + rE * u)
        vb = ADV * vb - (damp * lv + rE * v)
        return hbar, ub, vb, rd

    def keep_cot(L, St, k, lh, lu, lv):
        u = L("u%d" % k)
        St("lh%d" % k, lh)
        St("lu%d" % k, lu)
        St("lv%d" % k, lv)
        St("uu%d" % k, u * lu)
        St("uv%d" % k, u * lv)

    def add_drag(L, St, rd):
        St("acc", L("acc") - rd / (2.0 * L("c")))

    bb = [-(-(10 - 2 * k) // 8) for k in range(6)]
    for n in (1, 0):
        s, a, b = 3 * n, 3 * n + 1, 3 * n + 2
        top = n == 1

        def from_b(L, St):
            hbar, ub, vb, rd = pull(L, b, not top)
            add_drag(L, St, rd)
            quarter = 0.25 * L("w")
            new = [hbar if top else hbar + L("lh%d" % b), ub + L("lu%d" % b), vb + L("lv%d" % b)]
            keep_cot(L, St, a, *[quarter * x for x in new])

        sweep(bb[5 - b], from_b)

        def from_a(L, St):
            w = L("w")
            hbar, ub, vb, rd = pull(L, a, True)
            add_drag(L, St, rd)
            keep_cot(L, St, s, *[w * (x + L(y + str(a))) for x, y in zip((hbar, ub, vb), ("lh", "lu", "lv"))])

        sweep(bb[5 - a], from_a)

        def from_s(L, St):
            hbar, ub, vb, rd = pull(L, s, True)
            add_drag(L, St, rd)
            new = []
            for x, value in (("lh", hbar), ("lu", ub), ("lv", vb)):
                total = value + L(x + str(s)) + 3.0 * L(x + str(a))
                if not (top and x == "lh"):
                    total = total + 0.5 * L(x + str(b))
                new.append(total)
            if top:
                scale = (2.0 / 3.0) * L("w")
                keep_cot(L, St, 2, *[scale * x for x in new])
            else:
                for name, value in zip(("oh", "ou", "ov"), new):
                    St(name, value)

        sweep(bb[5 - s], from_s)

    shape = (2 * LANES, LANES)
    gather = column_at(shape, 0) == lax.broadcasted_iota(jnp.int32, shape, 1) + HALO
    gather = jnp.where(gather, 1.0, 0.0).astype(jnp.bfloat16)

    lane = lax.broadcasted_iota(jnp.int32, (rows, LANES), 1)
    in_tile = jnp.logical_and(lane >= HALO // 2, lane < (HALO + LANES) // 2)

    def own_columns(name):
        planes = [jnp.where(in_tile, S[at[name], t, OWN : OWN + rows, :], 0.0) for t in range(2)]
        return pick(jnp.concatenate(planes, axis=1), gather)

    for i, name in enumerate(("oh", "ou", "ov")):
        adj_ref[i] = own_columns(name)
    grad = own_columns("acc")
    grad_ref[...] = grad
    farm_copy.wait()
    matched = farm_here[...] == place_x * ny + place_y
    scale = 1.0 / (rows * LANES)
    for ref, part in ((own_sum_ref, jnp.where(matched, grad, 0.0)), (other_sum_ref, jnp.where(matched, 0.0, grad))):
        total = jnp.sum(jnp.sum(part, axis=0, keepdims=True), axis=1, keepdims=True) * scale
        ref[...] = jnp.broadcast_to(total, (1, LANES))


def shards(elevation, velocity, depth, turbine, wet_tiles, farm):
    rows = elevation.shape[0]
    counts = (lax.axis_size("gx"), lax.axis_size("gy"))
    nx, ny = counts
    elev = elevation.reshape(rows, LANES)
    vel = velocity.reshape(2, rows, LANES)
    dep = depth.reshape(rows, LANES)
    turb = turbine.reshape(rows, LANES)
    farm_local = farm.reshape(rows, LANES)
    pairs_x = pairings(nx)
    pairs_y = pairings(ny)
    f32 = jnp.float32
    square = jax.ShapeDtypeStruct((LANES, LANES), f32)
    side = jax.ShapeDtypeStruct((rows, LANES), f32)
    corner = jax.ShapeDtypeStruct((HALO, LANES), f32)
    vmem = pl.BlockSpec(memory_space=pltpu.VMEM)
    shapes = [square] * len(pairs_x) + [side] * len(pairs_y) + [corner] * (len(pairs_x) * len(pairs_y))
    shapes.append(jax.ShapeDtypeStruct((8, LANES), f32))
    sent = pl.pallas_call(
        lambda *refs: pack_kernel(counts, *refs),
        out_shape=shapes,
        in_specs=[vmem] * 5 + [pl.BlockSpec(memory_space=pl.ANY)],
        out_specs=[vmem] * len(shapes),
        name="pack",
    )(wet_tiles, elev, vel, dep, turb, farm_local)
    sent = list(sent)
    wet = sent.pop()
    row_got = [lax.ppermute(sent.pop(0), "gx", list(enumerate(p))) for p in pairs_x]
    side_got = [lax.ppermute(sent.pop(0), "gy", list(enumerate(p))) for p in pairs_y]
    corner_got = [
        [
            lax.ppermute(
                sent.pop(0),
                ("gx", "gy"),
                [(i * ny + j, px[i] * ny + py[j]) for i in range(nx) for j in range(ny)],
            )
            for py in pairs_y
        ]
        for px in pairs_x
    ]

    def left_right(got):
        if len(got) == 1:
            return got
        odd = lax.rem(lax.axis_index("gy"), 2) == 1
        return [jnp.where(odd, got[0], got[1]), jnp.where(odd, got[1], got[0])]

    edges = left_right(side_got)
    corners = [c for got in corner_got for c in left_right(got)]
    n_in = 6 + len(row_got) + len(edges) + len(corners)
    planes = 4 + 6 * 17 + 4
    adjoint, grad, own_sum, other_sum = pl.pallas_call(
        lambda *refs: main_kernel(counts, *refs),
        out_shape=[
            jax.ShapeDtypeStruct((3, rows, LANES), f32),
            side,
            jax.ShapeDtypeStruct((1, LANES), f32),
            jax.ShapeDtypeStruct((1, LANES), f32),
        ],
        in_specs=[vmem] * 5 + [pl.BlockSpec(memory_space=pl.ANY)] + [vmem] * (n_in - 6),
        out_specs=[vmem] * 4,
        scratch_shapes=[
            pltpu.VMEM((planes, 2, rows + 2 * OWN, LANES), f32),
            pltpu.VMEM((rows, LANES), jnp.int32),
            pltpu.SemaphoreType.DMA,
        ],
        compiler_params=pltpu.CompilerParams(vmem_limit_bytes=40 * 1024 * 1024),
        name="adjoint",
    )(wet, elev, vel, dep, turb, farm_local, *row_got, *edges, *corners)
    passed = lax.ppermute(other_sum, "gx", [(i, (i + 1) % nx) for i in range(nx)])
    return (
        adjoint.reshape((3,) + elevation.shape),
        grad.reshape(elevation.shape),
        (own_sum + passed)[0, :1],
    )


def solution(mesh):
    in_specs = (
        P("gx", None, "gy", None),
        P(None, "gx", None, "gy", None),
        P("gx", None, "gy", None),
        P("gx", None, "gy", None),
        P("gx", None, "gy"),
        P("gx", None, "gy", None),
    )
    out_specs = (P(None, "gx", None, "gy", None), P("gx", None, "gy", None), P(("gx", "gy")))
    return jax.shard_map(shards, mesh=mesh, in_specs=in_specs, out_specs=out_specs, check_vma=False)
```

```python
import jax
import jax.numpy as jnp
from jax import lax
from jax.experimental import pallas as pl
from jax.experimental.pallas import tpu as pltpu
from jax.sharding import PartitionSpec as P

SPEED_EPS = 0.01
BED_DRAG = 0.1
LANES = 128
HALO = 24
GUARD = 8
OWN = GUARD + HALO
FIELDS = 5
STEP = 16
VMEM_MAIN = 36 * 1024 * 1024
VMEM_OWN = 36 * 1024 * 1024
VMEM_LAST = 12 * 1024 * 1024
WIDE = LANES + 2 * HALO
ADV = 0.1 / 12.0
GRAV_RATIO = 3.0
VISC = 0.004 / ADV
EDGE = 4


def pairings(count):
    even = [i ^ 1 for i in range(count)]
    if count == 2:
        return [even]
    odd = [i if i in (0, count - 1) else ((i + 1) ^ 1) - 1 for i in range(count)]
    return [even, odd]


def roles(axis, count):
    place = lax.axis_index(axis)
    odd = lax.rem(place, 2)
    after_a = 1 - odd
    result = [(after_a, True)]
    if count > 2:
        after_b = odd
        exists = jnp.where(after_b == 1, place < count - 1, place > 0)
        result.append((after_b, exists))
    return result


def pack_kernel(counts, wet_ref, elev_ref, vel_ref, depth_ref, turb_ref, farm_ref, *outs):
    rows = elev_ref.shape[0]
    fields = [elev_ref[...], vel_ref[0], vel_ref[1], depth_ref[...], turb_ref[...]]
    refs = [elev_ref, vel_ref.at[0], vel_ref.at[1], depth_ref, turb_ref]
    wet = wet_ref[0].astype(jnp.float32)
    roles_x = roles("gx", counts[0])
    roles_y = roles("gy", counts[1])
    outs = list(outs)
    stack = outs.pop()
    for f, field in enumerate(fields):
        stack[rows * f : rows * (f + 1), :] = field
    own = lax.axis_index("gx") * counts[1] + lax.axis_index("gy")
    stack[rows * FIELDS : rows * (FIELDS + 1), :] = jnp.where(farm_ref[...] == own, 1.0, 0.0)
    stack[rows * (FIELDS + 1) :, :] = jnp.broadcast_to(wet, (8, LANES))
    row_outs = [outs.pop(0) for _ in roles_x]
    side_outs = [outs.pop(0) for _ in roles_y]
    starts = [pl.multiple_of(after * (rows - HALO), 8) for after, _ in roles_x]
    for start, out in zip(starts, row_outs):
        for f, ref in enumerate(refs):
            out[HALO * f : HALO * (f + 1), :] = ref[pl.ds(start, HALO), :]
        out[HALO * FIELDS :, :] = jnp.broadcast_to(wet, (LANES - HALO * FIELDS, LANES))
    lane = lax.broadcasted_iota(jnp.int32, (rows, LANES), 1)
    for (after, _), out in zip(roles_y, side_outs):
        packed = jnp.broadcast_to(wet, (rows, LANES))
        for f in reversed(range(FIELDS)):
            moved = jnp.where(
                after == 1,
                pltpu.roll(fields[f], HALO * (f + 1), 1),
                pltpu.roll(fields[f], HALO * f, 1),
            )
            packed = jnp.where(lane < HALO * (f + 1), moved, packed)
        out[...] = packed
    for start in starts:
        for side in side_outs:
            outs.pop(0)[...] = side[pl.ds(start, HALO), :]


class Pair:
    def __init__(self, even, odd):
        self.even, self.odd = even, odd

    def map(self, function):
        return Pair(function(self.even), function(self.odd))

    def __add__(self, other):
        return both(self, other, lambda a, b: a + b)

    def __sub__(self, other):
        return both(self, other, lambda a, b: a - b)

    def __mul__(self, other):
        return both(self, other, lambda a, b: a * b)

    def __truediv__(self, other):
        return both(self, other, lambda a, b: a / b)

    def __rmul__(self, other):
        return self.map(lambda a: other * a)


def both(a, b, function):
    if isinstance(b, Pair):
        return Pair(function(a.even, b.even), function(a.odd, b.odd))
    return Pair(function(a.even, b), function(a.odd, b))


def after(x):
    return pltpu.roll(x, LANES - 1, 1)


def before(x):
    return pltpu.roll(x, 1, 1)


def d_cols(f):
    ea, eb, oa, ob = after(f.even), before(f.even), after(f.odd), before(f.odd)
    slope = Pair(
        8.0 * (f.odd - ob) - (ea - eb),
        8.0 * (ea - f.even) - (oa - ob),
    )
    return slope, Pair(ea + eb, oa + ob)


def combine(p1, m1, p2, m2):
    return Pair(
        (p1.odd - after(p2.even)) - before(m1.odd - m2.even),
        (after(p1.even - p2.odd) - m1.even) + before(m2.odd),
    )


def thirds(x):
    one = x.astype(jnp.bfloat16)
    rest = x - one.astype(jnp.float32)
    two = rest.astype(jnp.bfloat16)
    three = (rest - two.astype(jnp.float32)).astype(jnp.bfloat16)
    return one, two, three


def pick(parts, chosen):
    got = [jnp.dot(part, chosen, preferred_element_type=jnp.float32) for part in parts]
    return (got[0] + got[1]) + got[2]


def column_at(shape, dim):
    place = lax.broadcasted_iota(jnp.int32, shape, dim)
    return 2 * lax.rem(place, LANES) + lax.div(place, LANES)


def own_columns(rows, planes):
    shape = (2 * LANES, LANES)
    gather = column_at(shape, 0) == lax.broadcasted_iota(jnp.int32, shape, 1) + HALO
    gather = jnp.where(gather, 1.0, 0.0).astype(jnp.bfloat16)
    lane = lax.broadcasted_iota(jnp.int32, (rows, LANES), 1)
    in_tile = jnp.logical_and(lane >= HALO // 2, lane < (HALO + LANES) // 2)
    both_planes = jnp.concatenate([jnp.where(in_tile, x, 0.0) for x in planes], axis=1)
    return pick(thirds(both_planes), gather)


def place_of(names, ref):
    return {name: (ref, i) for i, name in enumerate(names)}


SAVED = ("u", "v", "H", "xu", "xv", "yu", "yv", "dm", "om", "E", "rH")
COTANGENT = ("lh", "lu", "lv", "uu", "uv")
KEPT = [x + "0" for x in SAVED + COTANGENT] + [x + k for k in "12" for x in ("lh", "lu", "lv")]
PLANES = (
    ["w", "w25", "w75", "w13", "w23", "T", "c", "d", "power", "acc", "h0", "F0"]
    + [x + k for k in "12345" for x in ("h", "F") + SAVED]
    + [x + k for k in "12" for x in ("uu", "uv")]
    + [x + k for k in "345" for x in COTANGENT]
)


def sweep(at, rows, beyond, body):
    beyond = -(-beyond // EDGE) * EDGE
    stop = OWN + rows + beyond
    for start in range(OWN - beyond, stop, STEP):
        n = min(STEP, stop - start)

        def load(name, s=0):
            ref, i = at[name]
            return Pair(*[ref[i, t, start + s : start + s + n, :] for t in range(2)])

        def store(name, value):
            ref, i = at[name]
            ref[i, 0, start : start + n, :] = value.even
            ref[i, 1, start : start + n, :] = value.odd

        body(load, store)


def d_rows(L, name):
    p1, m1, p2, m2 = L(name, 1), L(name, -1), L(name, 2), L(name, -2)
    return 8.0 * (p1 - m1) - (p2 - m2), p1 + m1, p2 + m2


def tend(L, St, k, with_h):
    u, v, H, h = L("u%d" % k), L("v%d" % k), L("H%d" % k), L("h%d" % k)
    xu, su, tu = d_rows(L, "u%d" % k)
    xv, sv, tv = d_rows(L, "v%d" % k)
    yu, ru = d_cols(u)
    yv, rv = d_cols(v)
    near_u = (2.0 * VISC) * (su - 4.0 * u)
    near_v = (2.0 * VISC) * (sv - 4.0 * v)
    ring = Pair(near_u.odd + before(near_u.odd), near_u.even + after(near_u.even))
    bu = (VISC * ((tu + ru) - 12.0 * u) - 4.0 * near_u) + ring
    bv = VISC * ((tv + rv) - 12.0 * v) - 4.0 * near_v
    far = 8.0 * h
    yh = combine(far + near_v, far - near_v, h, h)
    xh = d_rows(L, "h%d" % k)[0]
    q2 = (u * u + v * v) + SPEED_EPS
    rH = H.map(lambda x: 1.0 / x)
    E = L("c") * (q2.map(lax.rsqrt) * rH)
    damp = E * q2
    om = damp.map(lambda x: 1.0 - x)
    for name, value in (
        ("xu", xu), ("xv", xv), ("yu", yu), ("yv", yv), ("dm", damp), ("om", om), ("E", E), ("rH", rH),
    ):
        St(name + str(k), value)
    eu = ((u * xu + v * yu) + xh) + bu
    ev = ((u * xv + v * yv) + yh) + bv
    if not with_h:
        return None, eu, ev, om
    return d_rows(L, "F%d" % k)[0] + d_cols(H * v)[0], eu, ev, om


def moved(L, St, k, with_h):
    eh, eu, ev, om = tend(L, St, k, with_h)
    return (
        L("h%d" % k) - ADV * eh if with_h else None,
        om * L("u%d" % k) - ADV * eu,
        om * L("v%d" % k) - ADV * ev,
    )


def pull(L, k, with_h):
    u, v, H = L("u%d" % k), L("v%d" % k), L("H%d" % k)
    lu, lv = L("lu%d" % k), L("lv%d" % k)
    om, E, rH = L("om%d" % k), L("E%d" % k), L("rH%d" % k)
    xlu, su, tu = d_rows(L, "lu%d" % k)
    _, sv, tv = d_rows(L, "lv%d" % k)
    ylv, rv = d_cols(lv)
    vl = v * lu
    vl8, near, lu_s = 8.0 * vl, (2.0 * VISC) * (su - 4.0 * lu), VISC * lu
    ub = combine(vl8 - near, vl8 + near, vl + lu_s, vl - lu_s)
    ub = ub - (VISC * (tu - 12.0 * lu) - 4.0 * near)
    vl = v * lv
    vl8, near = 8.0 * vl, (2.0 * VISC) * (sv - 4.0 * lv)
    vb = combine(vl8 - near, vl8 + near, vl, vl)
    vb = vb - (VISC * ((tv + rv) - 12.0 * lv) - 4.0 * near)
    ub = ub + d_rows(L, "uu%d" % k)[0] - lu * L("xu%d" % k) - lv * L("xv%d" % k)
    vb = vb + d_rows(L, "uv%d" % k)[0] - lu * L("yu%d" % k) - lv * L("yv%d" % k)
    r = lu * u + lv * v
    rd = r * L("dm%d" % k)
    rE = r * E
    hb = xlu + ylv
    if with_h:
        lh = L("lh%d" % k)
        xlh = d_rows(L, "lh%d" % k)[0]
        ylh = d_cols(lh)[0]
        ub = ub + H * xlh
        vb = vb + H * ylh
        hb = hb + (u * xlh + v * ylh)
    hb = ADV * hb + rd * rH
    if with_h:
        hb = hb + lh
    ub = ADV * ub + (om * lu - rE * u)
    vb = ADV * vb + (om * lv - rE * v)
    return (hb, ub, vb), rd


def step_back(L, s, top):
    new, rd = pull(L, s, True)
    total = []
    for x, value in zip(("lh", "lu", "lv"), new):
        value = value + 3.0 * L(x + str(s + 1))
        if not (top and x == "lh"):
            value = value + 0.5 * L(x + str(s + 2))
        total.append(value)
    return total, rd


def last_kernel(kept_ref, adj_ref, last_ref):
    rows = adj_ref.shape[1]
    at = place_of(KEPT, kept_ref)
    at.update(place_of(["oh", "ou", "ov"], last_ref))

    def body(L, St):
        total, _ = step_back(L, 0, False)
        St("oh", GRAV_RATIO * total[0])
        St("ou", total[1])
        St("ov", total[2])

    sweep(at, rows, 0, body)
    for i in range(3):
        adj_ref[i] = own_columns(rows, [last_ref[i, t, OWN : OWN + rows, :] for t in range(2)])


def spread_matrix():
    shape = (LANES, 2 * LANES)
    hit = lax.broadcasted_iota(jnp.int32, shape, 0) + HALO == column_at(shape, 1)
    return jnp.where(hit, 1.0, 0.0).astype(jnp.bfloat16)


def own_kernel(stack_ref, planes_ref, flags_ref):
    rows = planes_ref.shape[2]
    chosen = spread_matrix()
    for f in range(FIELDS):
        value = pick(thirds(stack_ref[rows * f : rows * (f + 1), :]), chosen)
        for t in range(2):
            planes_ref[f, t] = value[:, LANES * t : LANES * (t + 1)]
    flags_ref[...] = stack_ref[rows * FIELDS :, :]


def main_kernel(counts, own_ref, flags_ref, *rest):
    rows = flags_ref.shape[0] - 8
    rest = list(rest)
    nx, ny = counts
    roles_x = roles("gx", nx)
    row_in = [rest.pop(0) for _ in roles_x]
    sides = 1 if ny == 2 else 2
    side_in = [rest.pop(0) for _ in range(sides)]
    corner_in = [[rest.pop(0) for _ in range(sides)] for _ in roles_x]
    grad_ref, own_sum_ref, other_sum_ref, kept_ref, S = rest
    place_y = lax.axis_index("gy")
    has_left = place_y > 0
    has_right = place_y < ny - 1
    wet = flags_ref[rows : rows + 1, :1]

    at = place_of(PLANES, S)
    at.update(place_of(KEPT, kept_ref))

    def spread(f):
        shape = (LANES, 2 * LANES)
        target = column_at(shape, 1)
        source = lax.broadcasted_iota(jnp.int32, shape, 0)
        blocks = []
        edge = source - HALO * f
        inside = jnp.logical_and(edge >= 0, edge < HALO)
        if sides == 1:
            offset = jnp.where(has_left, 0, LANES + HALO)
            blocks.append(jnp.logical_and(inside, edge + offset == target))
        else:
            hit_left = jnp.logical_and(inside, edge == target)
            hit_right = jnp.logical_and(inside, edge + (LANES + HALO) == target)
            blocks.append(jnp.logical_and(hit_left, has_left))
            blocks.append(jnp.logical_and(hit_right, has_right))
        return jnp.concatenate(
            [jnp.where(b, 1.0, 0.0).astype(jnp.bfloat16) for b in blocks], axis=0
        )

    edge_chosen = [spread(f) for f in range(FIELDS)]
    own_chosen = spread_matrix()

    def put(start, n, centre, edges, wet_centre, exists):
        column = column_at((n, 2 * LANES), 1)
        in_left = column < HALO
        in_right = column >= LANES + HALO
        known = jnp.logical_and(
            jnp.logical_or(jnp.logical_not(in_left), has_left),
            jnp.logical_or(jnp.logical_not(in_right), has_right),
        )
        known = jnp.logical_and(known, column < WIDE)
        if exists is not True:
            known = jnp.logical_and(known, exists)
        edge_parts = [thirds(x) for x in edges]

        edge_parts = [jnp.concatenate([x[i] for x in edge_parts], axis=1) for i in range(3)]

        def extended(f):
            if centre is None:
                value = pick(edge_parts, edge_chosen[f])
                value = value + jnp.concatenate([own_ref[f, 0], own_ref[f, 1]], axis=1)
            else:
                parts = [jnp.concatenate(x, axis=1) for x in zip(thirds(centre(f)), edge_parts)]
                value = pick(parts, jnp.concatenate([own_chosen, edge_chosen[f]], axis=0))
            return jnp.where(known, value, 1.0 if f == 3 else 0.0)

        values = [extended(f) for f in range(FIELDS)]
        wet_left = jnp.broadcast_to(edges[0][:, LANES - 1 :], (n, 2 * LANES))
        wet_right = jnp.broadcast_to(edges[-1][:, LANES - 1 :], (n, 2 * LANES))
        w = jnp.where(in_left, wet_left, jnp.where(in_right, wet_right, wet_centre))
        w = jnp.where(known, w, 0.0)
        h, u, v, d, turb = values
        h, d = GRAV_RATIO * h, GRAV_RATIO * d
        height = d + h
        planes = (
            ("w", w), ("w25", 0.25 * w), ("w75", 0.75 * w), ("w13", (1.0 / 3.0) * w), ("w23", (2.0 / 3.0) * w),
            ("T", turb), ("c", (0.5 * GRAV_RATIO) * (BED_DRAG + turb)), ("d", d),
            ("h0", h), ("u0", u), ("v0", v), ("H0", height), ("F0", height * u),
        )
        for name, value in planes:
            ref, i = at[name]
            for t in range(2):
                ref[i, t, pl.ds(start, n), :] = value[:, LANES * t : LANES * (t + 1)]

    put(OWN, rows, None, [x[...] for x in side_in], jnp.broadcast_to(wet, (rows, 2 * LANES)), True)
    for (partner_after, exists), rin, corners in zip(roles_x, row_in, corner_in):
        put(
            pl.multiple_of(GUARD + partner_after * (rows + HALO), 8),
            HALO,
            lambda f: rin[HALO * f : HALO * (f + 1), :],
            [x[...] for x in corners],
            jnp.broadcast_to(rin[LANES - 1 :, :1], (HALO, 2 * LANES)),
            exists,
        )

    def keep_state(L, St, k, h, u, v):
        H = L("d") + h
        St("h%d" % k, h)
        St("u%d" % k, u)
        St("v%d" % k, v)
        St("H%d" % k, H)
        St("F%d" % k, H * u)

    for n in range(2):
        s, a, b = 3 * n, 3 * n + 1, 3 * n + 2

        def first(L, St):
            w = L("w")
            keep_state(L, St, a, *[w * x for x in moved(L, St, s, True)])

        sweep(at, rows, HALO - 2 - 2 * s, first)

        def second(L, St):
            old, new = L("w75"), L("w25")
            state = [L(x + str(s)) for x in "huv"]
            keep_state(L, St, b, *[old * x + new * y for x, y in zip(state, moved(L, St, a, True))])

        sweep(at, rows, HALO - 2 - 2 * a, second)

        def third(L, St):
            old, new = L("w13"), L("w23")
            h, u, v = moved(L, St, b, n == 0)
            u = old * L("u%d" % s) + new * u
            v = old * L("v%d" % s) + new * v
            if n == 0:
                keep_state(L, St, 3, old * L("h0") + new * h, u, v)
                return
            q2 = (u * u + v * v) + SPEED_EPS
            q = q2.map(jnp.sqrt)
            w = L("w")
            St("power", w * (q2 * q))
            fac = (3.0 * new) * (L("T") * w * q)
            lu, lv = fac * u, fac * v
            ub = L("u5")
            St("lu5", lu)
            St("lv5", lv)
            St("uu5", ub * lu)
            St("uv5", ub * lv)

        sweep(at, rows, HALO - 2 - 2 * b, third)

    def keep_cot(L, St, k, lh, lu, lv):
        u = L("u%d" % k)
        St("lh%d" % k, lh)
        St("lu%d" % k, lu)
        St("lv%d" % k, lv)
        St("uu%d" % k, u * lu)
        St("uv%d" % k, u * lv)

    for n in (1, 0):
        s, a, b = 3 * n, 3 * n + 1, 3 * n + 2
        top = n == 1

        def from_b(L, St):
            new, rd = pull(L, b, not top)
            St("acc", rd if top else L("acc") + rd)
            quarter = L("w25")
            keep_cot(L, St, a, *[quarter * x for x in new])

        sweep(at, rows, 2 * b, from_b)

        def from_a(L, St):
            new, rd = pull(L, a, True)
            w = L("w")
            lh, lu, lv = [w * x for x in new]
            if not top:
                rd = rd + (lu * L("u0") + lv * L("v0")) * L("dm0")
            St("acc", L("acc") + rd)
            keep_cot(L, St, s, lh, lu, lv)

        sweep(at, rows, 2 * a, from_a)

        def from_s(L, St):
            total, rd = step_back(L, s, True)
            St("acc", L("acc") + rd)
            scale = L("w23")
            keep_cot(L, St, 2, *[scale * x for x in total])

        if top:
            sweep(at, rows, 2 * s, from_s)

    def own_rows(name):
        ref, i = at[name]
        return [ref[i, t, OWN : OWN + rows, :] for t in range(2)]

    share = [
        p - a / (BED_DRAG + t) for p, a, t in zip(own_rows("power"), own_rows("acc"), own_rows("T"))
    ]
    grad = own_columns(rows, share)
    grad_ref[...] = grad
    matched = flags_ref[:rows, :] > 0.5
    scale = 1.0 / (rows * LANES)
    for ref, part in ((own_sum_ref, jnp.where(matched, grad, 0.0)), (other_sum_ref, jnp.where(matched, 0.0, grad))):
        total = jnp.sum(jnp.sum(part, axis=0, keepdims=True), axis=1, keepdims=True) * scale
        ref[...] = jnp.broadcast_to(total, (1, LANES))


def shards(elevation, velocity, depth, turbine, wet_tiles, farm):
    rows = elevation.shape[0]
    counts = (lax.axis_size("gx"), lax.axis_size("gy"))
    nx, ny = counts
    elev = elevation.reshape(rows, LANES)
    vel = velocity.reshape(2, rows, LANES)
    dep = depth.reshape(rows, LANES)
    turb = turbine.reshape(rows, LANES)
    farm_local = farm.reshape(rows, LANES)
    pairs_x = pairings(nx)
    pairs_y = pairings(ny)
    f32 = jnp.float32
    square = jax.ShapeDtypeStruct((LANES, LANES), f32)
    side = jax.ShapeDtypeStruct((rows, LANES), f32)
    corner = jax.ShapeDtypeStruct((HALO, LANES), f32)
    vmem = pl.BlockSpec(memory_space=pltpu.VMEM)
    shapes = [square] * len(pairs_x) + [side] * len(pairs_y) + [corner] * (len(pairs_x) * len(pairs_y))
    shapes.append(jax.ShapeDtypeStruct((rows * (FIELDS + 1) + 8, LANES), f32))
    sent = pl.pallas_call(
        lambda *refs: pack_kernel(counts, *refs),
        out_shape=shapes,
        in_specs=[vmem] * 6,
        out_specs=[vmem] * len(shapes),
        name="pack",
    )(wet_tiles, elev, vel, dep, turb, farm_local)
    sent = list(sent)
    stack = sent.pop()
    row_got = [lax.ppermute(sent.pop(0), "gx", list(enumerate(p))) for p in pairs_x]
    side_got = [lax.ppermute(sent.pop(0), "gy", list(enumerate(p))) for p in pairs_y]
    corner_got = [
        [
            lax.ppermute(
                sent.pop(0),
                ("gx", "gy"),
                [(i * ny + j, px[i] * ny + py[j]) for i in range(nx) for j in range(ny)],
            )
            for py in pairs_y
        ]
        for px in pairs_x
    ]

    def left_right(got):
        if len(got) == 1:
            return got
        odd = lax.rem(lax.axis_index("gy"), 2) == 1
        return [jnp.where(odd, got[0], got[1]), jnp.where(odd, got[1], got[0])]

    edges = left_right(side_got)
    corners = [c for got in corner_got for c in left_right(got)]
    own_planes, flags = pl.pallas_call(
        own_kernel,
        out_shape=[
            jax.ShapeDtypeStruct((FIELDS, 2, rows, LANES), f32),
            jax.ShapeDtypeStruct((rows + 8, LANES), f32),
        ],
        in_specs=[vmem],
        out_specs=[vmem] * 2,
        compiler_params=pltpu.CompilerParams(vmem_limit_bytes=VMEM_OWN),
        cost_estimate=pl.CostEstimate(flops=4000000, bytes_accessed=6000000, transcendentals=0),
        name="own",
    )(stack)
    n_in = 2 + len(row_got) + len(edges) + len(corners)
    plane = (2, rows + 2 * OWN, LANES)
    grad, own_sum, other_sum, kept = pl.pallas_call(
        lambda *refs: main_kernel(counts, *refs),
        out_shape=[
            side,
            jax.ShapeDtypeStruct((1, LANES), f32),
            jax.ShapeDtypeStruct((1, LANES), f32),
            jax.ShapeDtypeStruct((len(KEPT),) + plane, f32),
        ],
        in_specs=[vmem] * n_in,
        out_specs=[vmem] * 4,
        scratch_shapes=[pltpu.VMEM((len(PLANES),) + plane, f32)],
        compiler_params=pltpu.CompilerParams(vmem_limit_bytes=VMEM_MAIN),
        name="adjoint",
    )(own_planes, flags, *row_got, *edges, *corners)
    passed = lax.ppermute(other_sum, "gx", [(i, (i + 1) % nx) for i in range(nx)])
    adjoint = pl.pallas_call(
        last_kernel,
        out_shape=jax.ShapeDtypeStruct((3, rows, LANES), f32),
        in_specs=[vmem],
        out_specs=vmem,
        scratch_shapes=[pltpu.VMEM((3,) + plane, f32)],
        compiler_params=pltpu.CompilerParams(vmem_limit_bytes=VMEM_LAST),
        cost_estimate=pl.CostEstimate(flops=4000000, bytes_accessed=6000000, transcendentals=0),
        name="last",
    )(kept)
    return (
        adjoint.reshape((3,) + elevation.shape),
        grad.reshape(elevation.shape),
        (own_sum + passed)[0, :1],
    )


def solution(mesh):
    in_specs = (
        P("gx", None, "gy", None),
        P(None, "gx", None, "gy", None),
        P("gx", None, "gy", None),
        P("gx", None, "gy", None),
        P("gx", None, "gy"),
        P("gx", None, "gy", None),
    )
    out_specs = (P(None, "gx", None, "gy", None), P("gx", None, "gy", None), P(("gx", "gy")))
    return jax.shard_map(shards, mesh=mesh, in_specs=in_specs, out_specs=out_specs, check_vma=False)
```

```python
import jax
import jax.numpy as jnp
from jax import lax
from jax.experimental import pallas as pl
from jax.experimental.pallas import tpu as pltpu
from jax.sharding import PartitionSpec as P

SPEED_EPS = 0.01
BED_DRAG = 0.1
LANES = 128
HALO = 24
GUARD = 8
OWN = GUARD + HALO
FIELDS = 5
STEP = 16
VMEM_MAIN = 36 * 1024 * 1024
VMEM_OWN = 36 * 1024 * 1024
VMEM_LAST = 12 * 1024 * 1024
WIDE = LANES + 2 * HALO
ADV = 0.1 / 12.0
GRAV_RATIO = 3.0
VISC = 0.004 / ADV
EDGE = 4


def pairings(count):
    even = [i ^ 1 for i in range(count)]
    if count == 2:
        return [even]
    odd = [i if i in (0, count - 1) else ((i + 1) ^ 1) - 1 for i in range(count)]
    return [even, odd]


def roles(axis, count):
    place = lax.axis_index(axis)
    odd = lax.rem(place, 2)
    after_a = 1 - odd
    result = [(after_a, True)]
    if count > 2:
        after_b = odd
        exists = jnp.where(after_b == 1, place < count - 1, place > 0)
        result.append((after_b, exists))
    return result


def pack_kernel(counts, wet_ref, elev_ref, vel_ref, depth_ref, turb_ref, farm_ref, *outs):
    rows = elev_ref.shape[0]
    fields = [elev_ref[...], vel_ref[0], vel_ref[1], depth_ref[...], turb_ref[...]]
    refs = [elev_ref, vel_ref.at[0], vel_ref.at[1], depth_ref, turb_ref]
    wet = wet_ref[0].astype(jnp.float32)
    roles_x = roles("gx", counts[0])
    roles_y = roles("gy", counts[1])
    outs = list(outs)
    stack = outs.pop()
    for f, field in enumerate(fields):
        stack[rows * f : rows * (f + 1), :] = field
    own = lax.axis_index("gx") * counts[1] + lax.axis_index("gy")
    stack[rows * FIELDS : rows * (FIELDS + 1), :] = jnp.where(farm_ref[...] == own, 1.0, 0.0)
    stack[rows * (FIELDS + 1) :, :] = jnp.broadcast_to(wet, (8, LANES))
    row_outs = [outs.pop(0) for _ in roles_x]
    side_outs = [outs.pop(0) for _ in roles_y]
    starts = [pl.multiple_of(after * (rows - HALO), 8) for after, _ in roles_x]
    for start, out in zip(starts, row_outs):
        for f, ref in enumerate(refs):
            out[HALO * f : HALO * (f + 1), :] = ref[pl.ds(start, HALO), :]
        out[HALO * FIELDS :, :] = jnp.broadcast_to(wet, (LANES - HALO * FIELDS, LANES))
    lane = lax.broadcasted_iota(jnp.int32, (rows, LANES), 1)
    for (after, _), out in zip(roles_y, side_outs):
        packed = jnp.broadcast_to(wet, (rows, LANES))
        for f in reversed(range(FIELDS)):
            moved = pltpu.roll(fields[f], HALO * (f + after), 1)
            packed = jnp.where(lane < HALO * (f + 1), moved, packed)
        out[...] = packed
    for start in starts:
        for side in side_outs:
            outs.pop(0)[...] = side[pl.ds(start, HALO), :]


class Pair:
    def __init__(self, even, odd):
        self.even, self.odd = even, odd

    def map(self, function):
        return Pair(function(self.even), function(self.odd))

    def __add__(self, other):
        return both(self, other, lambda a, b: a + b)

    def __sub__(self, other):
        return both(self, other, lambda a, b: a - b)

    def __mul__(self, other):
        return both(self, other, lambda a, b: a * b)

    def __truediv__(self, other):
        return both(self, other, lambda a, b: a / b)

    def __rmul__(self, other):
        return self.map(lambda a: other * a)


def both(a, b, function):
    if isinstance(b, Pair):
        return Pair(function(a.even, b.even), function(a.odd, b.odd))
    return Pair(function(a.even, b), function(a.odd, b))


def after(x):
    return pltpu.roll(x, LANES - 1, 1)


def before(x):
    return pltpu.roll(x, 1, 1)


def d_cols(f):
    ea, eb, oa, ob = after(f.even), before(f.even), after(f.odd), before(f.odd)
    slope = Pair(
        8.0 * (f.odd - ob) - (ea - eb),
        8.0 * (ea - f.even) - (oa - ob),
    )
    return slope, Pair(ea + eb, oa + ob)


def combine(p1, m1, p2, m2):
    return Pair(
        (p1.odd - after(p2.even)) - before(m1.odd - m2.even),
        (after(p1.even - p2.odd) - m1.even) + before(m2.odd),
    )


def thirds(x):
    one = x.astype(jnp.bfloat16)
    rest = x - one.astype(jnp.float32)
    two = rest.astype(jnp.bfloat16)
    three = (rest - two.astype(jnp.float32)).astype(jnp.bfloat16)
    return one, two, three


def pick(parts, chosen):
    got = [jnp.dot(part, chosen, preferred_element_type=jnp.float32) for part in parts]
    return (got[0] + got[1]) + got[2]


def column_at(shape, dim):
    place = lax.broadcasted_iota(jnp.int32, shape, dim)
    return 2 * lax.rem(place, LANES) + lax.div(place, LANES)


def own_columns(rows, planes):
    shape = (2 * LANES, LANES)
    gather = column_at(shape, 0) == lax.broadcasted_iota(jnp.int32, shape, 1) + HALO
    gather = jnp.where(gather, 1.0, 0.0).astype(jnp.bfloat16)
    lane = lax.broadcasted_iota(jnp.int32, (rows, LANES), 1)
    in_tile = jnp.logical_and(lane >= HALO // 2, lane < (HALO + LANES) // 2)
    both_planes = jnp.concatenate([jnp.where(in_tile, x, 0.0) for x in planes], axis=1)
    return pick(thirds(both_planes), gather)


def place_of(names, ref):
    return {name: (ref, i) for i, name in enumerate(names)}


SAVED = ("u", "v", "H", "xu", "xv", "yu", "yv", "dm", "om", "E", "rH")
COTANGENT = ("lh", "lu", "lv", "uu", "uv")
KEPT = [x + "0" for x in SAVED + COTANGENT] + [x + k for k in "12" for x in ("lh", "lu", "lv")]
PLANES = (
    ["w", "w25", "w75", "w13", "w23", "T", "c", "d", "power", "acc", "h0", "F0"]
    + [x + k for k in "12345" for x in ("h", "F") + SAVED]
    + [x + k for k in "12" for x in ("uu", "uv")]
    + [x + k for k in "345" for x in COTANGENT]
)


def sweep(at, rows, beyond, body):
    beyond = -(-beyond // EDGE) * EDGE
    stop = OWN + rows + beyond
    for start in range(OWN - beyond, stop, STEP):
        n = min(STEP, stop - start)

        def load(name, s=0):
            ref, i = at[name]
            return Pair(*[ref[i, t, start + s : start + s + n, :] for t in range(2)])

        def store(name, value):
            ref, i = at[name]
            ref[i, 0, start : start + n, :] = value.even
            ref[i, 1, start : start + n, :] = value.odd

        body(load, store)


def d_rows(L, name):
    p1, m1, p2, m2 = L(name, 1), L(name, -1), L(name, 2), L(name, -2)
    return 8.0 * (p1 - m1) - (p2 - m2), p1 + m1, p2 + m2


def tend(L, St, k, with_h):
    u, v, H, h = L("u%d" % k), L("v%d" % k), L("H%d" % k), L("h%d" % k)
    xu, su, tu = d_rows(L, "u%d" % k)
    xv, sv, tv = d_rows(L, "v%d" % k)
    yu, ru = d_cols(u)
    yv, rv = d_cols(v)
    near_u = (2.0 * VISC) * (su - 4.0 * u)
    near_v = (2.0 * VISC) * (sv - 4.0 * v)
    ring = Pair(near_u.odd + before(near_u.odd), near_u.even + after(near_u.even))
    bu = (VISC * ((tu + ru) - 12.0 * u) - 4.0 * near_u) + ring
    bv = VISC * ((tv + rv) - 12.0 * v) - 4.0 * near_v
    far = 8.0 * h
    yh = combine(far + near_v, far - near_v, h, h)
    xh = d_rows(L, "h%d" % k)[0]
    q2 = (u * u + v * v) + SPEED_EPS
    rH = H.map(lambda x: 1.0 / x)
    E = L("c") * (q2.map(lax.rsqrt) * rH)
    damp = E * q2
    om = damp.map(lambda x: 1.0 - x)
    for name, value in (
        ("xu", xu), ("xv", xv), ("yu", yu), ("yv", yv), ("dm", damp), ("om", om), ("E", E), ("rH", rH),
    ):
        St(name + str(k), value)
    eu = ((u * xu + v * yu) + xh) + bu
    ev = ((u * xv + v * yv) + yh) + bv
    if not with_h:
        return None, eu, ev, om
    return d_rows(L, "F%d" % k)[0] + d_cols(H * v)[0], eu, ev, om


def moved(L, St, k, with_h):
    eh, eu, ev, om = tend(L, St, k, with_h)
    return (
        L("h%d" % k) - ADV * eh if with_h else None,
        om * L("u%d" % k) - ADV * eu,
        om * L("v%d" % k) - ADV * ev,
    )


def pull(L, k, with_h):
    u, v, H = L("u%d" % k), L("v%d" % k), L("H%d" % k)
    lu, lv = L("lu%d" % k), L("lv%d" % k)
    om, E, rH = L("om%d" % k), L("E%d" % k), L("rH%d" % k)
    xlu, su, tu = d_rows(L, "lu%d" % k)
    _, sv, tv = d_rows(L, "lv%d" % k)
    ylv, rv = d_cols(lv)
    vl = v * lu
    vl8, near, lu_s = 8.0 * vl, (2.0 * VISC) * (su - 4.0 * lu), VISC * lu
    ub = combine(vl8 - near, vl8 + near, vl + lu_s, vl - lu_s)
    ub = ub - (VISC * (tu - 12.0 * lu) - 4.0 * near)
    vl = v * lv
    vl8, near = 8.0 * vl, (2.0 * VISC) * (sv - 4.0 * lv)
    vb = combine(vl8 - near, vl8 + near, vl, vl)
    vb = vb - (VISC * ((tv + rv) - 12.0 * lv) - 4.0 * near)
    ub = ub + d_rows(L, "uu%d" % k)[0] - lu * L("xu%d" % k) - lv * L("xv%d" % k)
    vb = vb + d_rows(L, "uv%d" % k)[0] - lu * L("yu%d" % k) - lv * L("yv%d" % k)
    r = lu * u + lv * v
    rd = r * L("dm%d" % k)
    rE = r * E
    hb = xlu + ylv
    if with_h:
        lh = L("lh%d" % k)
        xlh = d_rows(L, "lh%d" % k)[0]
        ylh = d_cols(lh)[0]
        ub = ub + H * xlh
        vb = vb + H * ylh
        hb = hb + (u * xlh + v * ylh)
    hb = ADV * hb + rd * rH
    if with_h:
        hb = hb + lh
    ub = ADV * ub + (om * lu - rE * u)
    vb = ADV * vb + (om * lv - rE * v)
    return (hb, ub, vb), rd


def step_back(L, s, top):
    new, rd = pull(L, s, True)
    total = []
    for x, value in zip(("lh", "lu", "lv"), new):
        value = value + 3.0 * L(x + str(s + 1))
        if not (top and x == "lh"):
            value = value + 0.5 * L(x + str(s + 2))
        total.append(value)
    return total, rd


def last_kernel(kept_ref, adj_ref, last_ref):
    rows = adj_ref.shape[1]
    at = place_of(KEPT, kept_ref)
    at.update(place_of(["oh", "ou", "ov"], last_ref))

    def body(L, St):
        total, _ = step_back(L, 0, False)
        St("oh", GRAV_RATIO * total[0])
        St("ou", total[1])
        St("ov", total[2])

    sweep(at, rows, 0, body)
    for i in range(3):
        adj_ref[i] = own_columns(rows, [last_ref[i, t, OWN : OWN + rows, :] for t in range(2)])


def spread_matrix():
    shape = (LANES, 2 * LANES)
    hit = lax.broadcasted_iota(jnp.int32, shape, 0) + HALO == column_at(shape, 1)
    return jnp.where(hit, 1.0, 0.0).astype(jnp.bfloat16)


def own_kernel(stack_ref, planes_ref, flags_ref):
    rows = planes_ref.shape[2]
    chosen = spread_matrix()
    for f in range(FIELDS):
        value = pick(thirds(stack_ref[rows * f : rows * (f + 1), :]), chosen)
        for t in range(2):
            planes_ref[f, t] = value[:, LANES * t : LANES * (t + 1)]
    flags_ref[...] = stack_ref[rows * FIELDS :, :]


def main_kernel(counts, own_ref, flags_ref, *rest):
    rows = flags_ref.shape[0] - 8
    rest = list(rest)
    nx, ny = counts
    roles_x = roles("gx", nx)
    row_in = [rest.pop(0) for _ in roles_x]
    sides = 1 if ny == 2 else 2
    side_in = [rest.pop(0) for _ in range(sides)]
    corner_in = [[rest.pop(0) for _ in range(sides)] for _ in roles_x]
    grad_ref, own_sum_ref, other_sum_ref, kept_ref, S = rest
    place_y = lax.axis_index("gy")
    has_left = place_y > 0
    has_right = place_y < ny - 1
    wet = flags_ref[rows : rows + 1, :1]

    at = place_of(PLANES, S)
    at.update(place_of(KEPT, kept_ref))

    def spread(f):
        shape = (LANES, 2 * LANES)
        target = column_at(shape, 1)
        source = lax.broadcasted_iota(jnp.int32, shape, 0)
        blocks = []
        edge = source - HALO * f
        inside = jnp.logical_and(edge >= 0, edge < HALO)
        if sides == 1:
            offset = jnp.where(has_left, 0, LANES + HALO)
            blocks.append(jnp.logical_and(inside, edge + offset == target))
        else:
            hit_left = jnp.logical_and(inside, edge == target)
            hit_right = jnp.logical_and(inside, edge + (LANES + HALO) == target)
            blocks.append(jnp.logical_and(hit_left, has_left))
            blocks.append(jnp.logical_and(hit_right, has_right))
        return jnp.concatenate(
            [jnp.where(b, 1.0, 0.0).astype(jnp.bfloat16) for b in blocks], axis=0
        )

    edge_chosen = [spread(f) for f in range(FIELDS)]
    own_chosen = spread_matrix()

    def put(start, n, centre, edges, wet_centre, exists):
        column = column_at((n, 2 * LANES), 1)
        in_left = column < HALO
        in_right = column >= LANES + HALO
        known = jnp.logical_and(
            jnp.logical_or(jnp.logical_not(in_left), has_left),
            jnp.logical_or(jnp.logical_not(in_right), has_right),
        )
        known = jnp.logical_and(known, column < WIDE)
        if exists is not True:
            known = jnp.logical_and(known, exists)
        edge_parts = [thirds(x) for x in edges]

        edge_parts = [jnp.concatenate([x[i] for x in edge_parts], axis=1) for i in range(3)]

        def extended(f):
            if centre is None:
                value = pick(edge_parts, edge_chosen[f])
                value = value + jnp.concatenate([own_ref[f, 0], own_ref[f, 1]], axis=1)
            else:
                parts = [jnp.concatenate(x, axis=1) for x in zip(thirds(centre(f)), edge_parts)]
                value = pick(parts, jnp.concatenate([own_chosen, edge_chosen[f]], axis=0))
            return jnp.where(known, value, 1.0 if f == 3 else 0.0)

        values = [extended(f) for f in range(FIELDS)]
        wet_left = jnp.broadcast_to(edges[0][:, LANES - 1 :], (n, 2 * LANES))
        wet_right = jnp.broadcast_to(edges[-1][:, LANES - 1 :], (n, 2 * LANES))
        w = jnp.where(in_left, wet_left, jnp.where(in_right, wet_right, wet_centre))
        w = jnp.where(known, w, 0.0)
        h, u, v, d, turb = values
        h, d = GRAV_RATIO * h, GRAV_RATIO * d
        height = d + h
        planes = (
            ("w", w), ("w25", 0.25 * w), ("w75", 0.75 * w), ("w13", (1.0 / 3.0) * w), ("w23", (2.0 / 3.0) * w),
            ("T", turb), ("c", (0.5 * GRAV_RATIO) * (BED_DRAG + turb)), ("d", d),
            ("h0", h), ("u0", u), ("v0", v), ("H0", height), ("F0", height * u),
        )
        for name, value in planes:
            ref, i = at[name]
            for t in range(2):
                ref[i, t, pl.ds(start, n), :] = value[:, LANES * t : LANES * (t + 1)]

    put(OWN, rows, None, [x[...] for x in side_in], jnp.broadcast_to(wet, (rows, 2 * LANES)), True)
    for (partner_after, exists), rin, corners in zip(roles_x, row_in, corner_in):
        put(
            pl.multiple_of(GUARD + partner_after * (rows + HALO), 8),
            HALO,
            lambda f: rin[HALO * f : HALO * (f + 1), :],
            [x[...] for x in corners],
            jnp.broadcast_to(rin[LANES - 1 :, :1], (HALO, 2 * LANES)),
            exists,
        )

    def keep_state(L, St, k, h, u, v):
        H = L("d") + h
        St("h%d" % k, h)
        St("u%d" % k, u)
        St("v%d" % k, v)
        St("H%d" % k, H)
        St("F%d" % k, H * u)

    for n in range(2):
        s, a, b = 3 * n, 3 * n + 1, 3 * n + 2

        def first(L, St):
            w = L("w")
            keep_state(L, St, a, *[w * x for x in moved(L, St, s, True)])

        sweep(at, rows, HALO - 2 - 2 * s, first)

        def second(L, St):
            old, new = L("w75"), L("w25")
            state = [L(x + str(s)) for x in "huv"]
            keep_state(L, St, b, *[old * x + new * y for x, y in zip(state, moved(L, St, a, True))])

        sweep(at, rows, HALO - 2 - 2 * a, second)

        def third(L, St):
            old, new = L("w13"), L("w23")
            h, u, v = moved(L, St, b, n == 0)
            u = old * L("u%d" % s) + new * u
            v = old * L("v%d" % s) + new * v
            if n == 0:
                keep_state(L, St, 3, old * L("h0") + new * h, u, v)
                return
            q2 = (u * u + v * v) + SPEED_EPS
            q = q2.map(jnp.sqrt)
            w = L("w")
            St("power", w * (q2 * q))
            fac = (3.0 * new) * (L("T") * w * q)
            lu, lv = fac * u, fac * v
            ub = L("u5")
            St("lu5", lu)
            St("lv5", lv)
            St("uu5", ub * lu)
            St("uv5", ub * lv)

        sweep(at, rows, HALO - 2 - 2 * b, third)

    def keep_cot(L, St, k, lh, lu, lv):
        u = L("u%d" % k)
        St("lh%d" % k, lh)
        St("lu%d" % k, lu)
        St("lv%d" % k, lv)
        St("uu%d" % k, u * lu)
        St("uv%d" % k, u * lv)

    for n in (1, 0):
        s, a, b = 3 * n, 3 * n + 1, 3 * n + 2
        top = n == 1

        def from_b(L, St):
            new, rd = pull(L, b, not top)
            St("acc", rd if top else L("acc") + rd)
            quarter = L("w25")
            keep_cot(L, St, a, *[quarter * x for x in new])

        sweep(at, rows, 2 * b, from_b)

        def from_a(L, St):
            new, rd = pull(L, a, True)
            w = L("w")
            lh, lu, lv = [w * x for x in new]
            if not top:
                rd = rd + (lu * L("u0") + lv * L("v0")) * L("dm0")
            St("acc", L("acc") + rd)
            keep_cot(L, St, s, lh, lu, lv)

        sweep(at, rows, 2 * a, from_a)

        def from_s(L, St):
            total, rd = step_back(L, s, True)
            St("acc", L("acc") + rd)
            scale = L("w23")
            keep_cot(L, St, 2, *[scale * x for x in total])

        if top:
            sweep(at, rows, 2 * s, from_s)

    def own_rows(name):
        ref, i = at[name]
        return [ref[i, t, OWN : OWN + rows, :] for t in range(2)]

    share = [
        p - a / (BED_DRAG + t) for p, a, t in zip(own_rows("power"), own_rows("acc"), own_rows("T"))
    ]
    grad = own_columns(rows, share)
    grad_ref[...] = grad
    matched = flags_ref[:rows, :] > 0.5
    scale = 1.0 / (rows * LANES)
    for ref, part in ((own_sum_ref, jnp.where(matched, grad, 0.0)), (other_sum_ref, jnp.where(matched, 0.0, grad))):
        total = jnp.sum(jnp.sum(part, axis=0, keepdims=True), axis=1, keepdims=True) * scale
        ref[...] = jnp.broadcast_to(total, (1, LANES))


def shards(elevation, velocity, depth, turbine, wet_tiles, farm):
    rows = elevation.shape[0]
    counts = (lax.axis_size("gx"), lax.axis_size("gy"))
    nx, ny = counts
    elev = elevation.reshape(rows, LANES)
    vel = velocity.reshape(2, rows, LANES)
    dep = depth.reshape(rows, LANES)
    turb = turbine.reshape(rows, LANES)
    farm_local = farm.reshape(rows, LANES)
    pairs_x = pairings(nx)
    pairs_y = pairings(ny)
    f32 = jnp.float32
    square = jax.ShapeDtypeStruct((LANES, LANES), f32)
    side = jax.ShapeDtypeStruct((rows, LANES), f32)
    corner = jax.ShapeDtypeStruct((HALO, LANES), f32)
    vmem = pl.BlockSpec(memory_space=pltpu.VMEM)
    shapes = [square] * len(pairs_x) + [side] * len(pairs_y) + [corner] * (len(pairs_x) * len(pairs_y))
    shapes.append(jax.ShapeDtypeStruct((rows * (FIELDS + 1) + 8, LANES), f32))
    sent = pl.pallas_call(
        lambda *refs: pack_kernel(counts, *refs),
        out_shape=shapes,
        in_specs=[vmem] * 6,
        out_specs=[vmem] * len(shapes),
        name="pack",
    )(wet_tiles, elev, vel, dep, turb, farm_local)
    sent = list(sent)
    stack = sent.pop()
    row_got = [lax.ppermute(sent.pop(0), "gx", list(enumerate(p))) for p in pairs_x]
    side_got = [lax.ppermute(sent.pop(0), "gy", list(enumerate(p))) for p in pairs_y]
    corner_got = [
        [
            lax.ppermute(
                sent.pop(0),
                ("gx", "gy"),
                [(i * ny + j, px[i] * ny + py[j]) for i in range(nx) for j in range(ny)],
            )
            for py in pairs_y
        ]
        for px in pairs_x
    ]

    def left_right(got):
        if len(got) == 1:
            return got
        odd = lax.rem(lax.axis_index("gy"), 2) == 1
        return [jnp.where(odd, got[0], got[1]), jnp.where(odd, got[1], got[0])]

    edges = left_right(side_got)
    corners = [c for got in corner_got for c in left_right(got)]
    own_planes, flags = pl.pallas_call(
        own_kernel,
        out_shape=[
            jax.ShapeDtypeStruct((FIELDS, 2, rows, LANES), f32),
            jax.ShapeDtypeStruct((rows + 8, LANES), f32),
        ],
        in_specs=[vmem],
        out_specs=[vmem] * 2,
        compiler_params=pltpu.CompilerParams(vmem_limit_bytes=VMEM_OWN),
        cost_estimate=pl.CostEstimate(flops=4000000, bytes_accessed=6000000, transcendentals=0),
        name="own",
    )(stack)
    n_in = 2 + len(row_got) + len(edges) + len(corners)
    plane = (2, rows + 2 * OWN, LANES)
    grad, own_sum, other_sum, kept = pl.pallas_call(
        lambda *refs: main_kernel(counts, *refs),
        out_shape=[
            side,
            jax.ShapeDtypeStruct((1, LANES), f32),
            jax.ShapeDtypeStruct((1, LANES), f32),
            jax.ShapeDtypeStruct((len(KEPT),) + plane, f32),
        ],
        in_specs=[vmem] * n_in,
        out_specs=[vmem] * 4,
        scratch_shapes=[pltpu.VMEM((len(PLANES),) + plane, f32)],
        compiler_params=pltpu.CompilerParams(vmem_limit_bytes=VMEM_MAIN),
        name="adjoint",
    )(own_planes, flags, *row_got, *edges, *corners)
    passed = lax.ppermute(other_sum, "gx", [(i, (i + 1) % nx) for i in range(nx)])
    adjoint = pl.pallas_call(
        last_kernel,
        out_shape=jax.ShapeDtypeStruct((3, rows, LANES), f32),
        in_specs=[vmem],
        out_specs=vmem,
        scratch_shapes=[pltpu.VMEM((3,) + plane, f32)],
        compiler_params=pltpu.CompilerParams(vmem_limit_bytes=VMEM_LAST),
        cost_estimate=pl.CostEstimate(flops=4000000, bytes_accessed=6000000, transcendentals=0),
        name="last",
    )(kept)
    return (
        adjoint.reshape((3,) + elevation.shape),
        grad.reshape(elevation.shape),
        (own_sum + passed)[0, :1],
    )


def solution(mesh):
    in_specs = (
        P("gx", None, "gy", None),
        P(None, "gx", None, "gy", None),
        P("gx", None, "gy", None),
        P("gx", None, "gy", None),
        P("gx", None, "gy"),
        P("gx", None, "gy", None),
    )
    out_specs = (P(None, "gx", None, "gy", None), P("gx", None, "gy", None), P(("gx", "gy")))
    return jax.shard_map(shards, mesh=mesh, in_specs=in_specs, out_specs=out_specs, check_vma=False)
```
